256 devices in a mesh: fsdp: 8 (over y, core), tp: 16 (over x_lo, z), rollout: 2 (over x_hi).
Axes of the slice: x: 4 (x_hi: 2, x_lo: 2; x = x_hi * 2 + x_lo), y: 4, z: 8, core: 2. Of those that a mesh axis runs over, the one named last changes fastest.
Arguments:
- weights: bfloat16 [2, 4096, 14336], P('rollout', 'fsdp', 'tp'), may hold values from -6 to 6
- gradient: bfloat16 [2, 4096, 14336], P('rollout', 'fsdp', 'tp'), may hold values from -6 to 6
- momentum: float32 [2, 4096, 14336], P('rollout', 'fsdp', 'tp'), may hold values from -90 to 90
- basis: float32 [2, 14336, 512], P('rollout', 'tp'), may hold values from -6 to 6
Outputs:
- weights_next: bfloat16 [2, 4096, 14336], P('rollout', 'fsdp', 'tp')
- momentum_next: float32 [2, 4096, 14336], P('rollout', 'fsdp', 'tp')
- basis_next: float32 [2, 14336, 512], P('rollout', 'tp')
- rollout_weights: bfloat16 [2, 4096, 14336], P(None, 'fsdp', 'tp')
The draws below stay inside these ranges and needn't reach their ends.
All inputs are finite; a program needn't handle non-finite values.
Results may differ from the reference program's by a relative error of at most 0.013.
Values may be sent and summed in bfloat16 or wider, within the bound.
No kernel may reach another device: no remote copies, remote signals or barrier semaphores. Data moves between devices by JAX's collectives and lax.ppermute only.
A program may use at most 64 MiB of HBM per device.

```python
import math
import jax
import jax.numpy as jnp
from jax import lax

ROWS = 4096
COLS = 14336
RANK = 512


def draw_momentum(key, part):
    key_base = jax.random.fold_in(key, 11)
    key_cols = jax.random.fold_in(key, 12)
    key_rows = jax.random.fold_in(key, 13)
    base = jnp.clip(jax.random.normal(key_base, (2, ROWS, COLS), jnp.float32), -6.0, 6.0)
    top = 10.0
    rising = jnp.exp(math.log(3.0) * jnp.arange(COLS, dtype=jnp.float32) / COLS)
    column_scale = jnp.exp(jax.random.uniform(key_cols, (2, 1, COLS), jnp.float32, 0.0, math.log(top))) * rising
    row_scale = jnp.exp(jax.random.uniform(key_rows, (2, ROWS, 1), jnp.float32, 0.0, math.log(4.0)))
    return base * column_scale * row_scale / 8.0


def level_of(rng, shape, pieces, least, top_value):
    loudness = 1.0
    for dim, shards_of in pieces:
        heights = jax.random.uniform(jax.random.fold_in(jax.random.fold_in(rng, 6), dim), (shards_of,), jnp.float32, least / len(pieces), top_value / len(pieces))
        loudness = loudness * jnp.repeat(jnp.exp(heights), shape[dim] // shards_of).reshape((-1,) + (1,) * (len(shape) - 1 - dim))
    return loudness


def scatter_about(own_key, extent, width, most, shards=(), kind=jnp.bfloat16):
    values = width * jax.random.normal(own_key, extent, jnp.float32)
    if shards:
        values = values * level_of(own_key, extent, shards, -0.22, 0.18)
    return jnp.clip(values, -most, most).astype(kind)


def setup_inputs(seed: int = 0) -> dict:
    splits = jax.random.split(jax.random.key(seed), 5)
    weights = scatter_about(splits[0], (2, ROWS, COLS), 1.0, 6.0, ((0, 2), (1, 8), (2, 16)))
    gradient = scatter_about(splits[1], (2, ROWS, COLS), 1.0, 6.0, ((0, 2), (1, 8), (2, 16)))
    momentum = draw_momentum(jax.random.fold_in(splits[4], 71), 0)
    basis = scatter_about(splits[3], (2, COLS, RANK), 1.0, 6.0, ((0, 2), (1, 16)), jnp.float32)
    return dict(weights=weights, gradient=gradient, momentum=momentum, basis=basis)


HIGH = lax.Precision.HIGHEST

def one_matrix(weight, grad, moment, prior):
    blend = moment + grad.astype(jnp.float32)
    left = jnp.dot(blend.astype(jnp.float32), prior.astype(jnp.float32), precision=HIGH, preferred_element_type=jnp.float32)
    gram = jnp.dot(left.T.astype(jnp.float32), left.astype(jnp.float32), precision=HIGH, preferred_element_type=jnp.float32)
    lower = jnp.linalg.cholesky(gram)
    ortho = lax.linalg.triangular_solve(lower, left, left_side=False, lower=True, transpose_a=True)
    right = jnp.dot(blend.T.astype(jnp.float32), ortho.astype(jnp.float32), precision=HIGH, preferred_element_type=jnp.float32)
    meansq = lax.optimization_barrier(jnp.sum(right * right, axis=0)) / COLS
    basis_new = right * lax.rsqrt(meansq + 1e-06)
    moment_new = blend - 0.05 * jnp.dot(ortho.astype(jnp.float32), right.T.astype(jnp.float32), precision=HIGH, preferred_element_type=jnp.float32)
    update = jnp.dot(ortho.astype(jnp.float32), basis_new.T.astype(jnp.float32), precision=HIGH, preferred_element_type=jnp.float32)
    weight_new = (weight.astype(jnp.float32) - 0.3 * update).astype(jnp.bfloat16)
    return (weight_new, moment_new, basis_new)

def reference(weights, gradient, momentum, basis):
    first = one_matrix(weights[0], gradient[0], momentum[0], basis[0])
    second = one_matrix(weights[1], gradient[1], momentum[1], basis[1])
    weights_next = jnp.stack([first[0], second[0]])
    momentum_next = jnp.stack([first[1], second[1]])
    basis_next = jnp.stack([first[2], second[2]])
    return (weights_next, momentum_next, basis_next, weights_next)
```

```python
import jax
import jax.numpy as jnp
from jax import lax
from jax.experimental import pallas as pl
from jax.experimental.pallas import tpu as pltpu
from jax.sharding import Mesh
from jax.sharding import PartitionSpec as P

COLS = 14336
TP = ("x", "z")
FSDP = ("y", "c")
F = jnp.float32
B = jnp.bfloat16

N = 512
NB = 128


def split(x):
    hi=x.astype(B); return hi,(x-hi.astype(F)).astype(B)
def dot3(a,b,dims):
    ah,al=split(a); bh,bl=split(b)
    d=lambda p,q: lax.dot_general(p,q,(dims,((),())),preferred_element_type=F)
    return d(ah,bh)+(d(ah,bl)+d(al,bh))

def factor(rows, inv_rows):
    n=len(rows)
    sub=lax.broadcasted_iota(jnp.int32,(8,NB),0)
    for p in range(n):
        for k in range(8):
            j=8*p+k
            col=jnp.broadcast_to(rows[p][:,j:j+1],(8,NB))
            rt=lax.rsqrt(col[k:k+1,:])
            row=rows[p][k:k+1,:]*rt
            erow=inv_rows[p][k:k+1,:]*rt
            row=jnp.broadcast_to(row,(8,NB)); erow=jnp.broadcast_to(erow,(8,NB))
            rtb=jnp.broadcast_to(rt,(8,NB))
            for q in range(p,n):
                c=col if q==p else jnp.broadcast_to(rows[q][:,j:j+1],(8,NB))
                l=c*rtb
                if q==p:
                    l=jnp.where(sub>k,l,0.0)
                    inv_rows[q]=jnp.where(sub==k,erow,inv_rows[q]-l*erow)
                else:
                    inv_rows[q]=inv_rows[q]-l*erow
                rows[q]=rows[q]-l*row
    return inv_rows

def chol_kernel(g_ref, left_ref, ortho_ref, w_ref, a_ref):
    a_ref[...]=g_ref[...]
    ri=lax.broadcasted_iota(jnp.int32,(8,NB),0); ci=lax.broadcasted_iota(jnp.int32,(8,NB),1)
    nblk=N//NB
    for k in range(nblk):
        lo=k*NB; hi=lo+NB
        rows=[a_ref[lo+8*p:lo+8*p+8,lo:hi] for p in range(NB//8)]
        inv=[(ci==ri+8*p).astype(F) for p in range(NB//8)]
        inv=factor(rows,inv)
        wkk=jnp.concatenate(inv,axis=0)
        w_ref[lo:hi,lo:hi]=wkk
        if hi<N: w_ref[lo:hi,hi:]=jnp.zeros((NB,N-hi),F)
        if k>0:
            w_ref[lo:hi,:lo]=dot3(wkk,w_ref[lo:hi,:lo],((1,),(0,)))
        if hi<N:
            r=dot3(wkk,a_ref[lo:hi,hi:],((1,),(0,)))
            a_ref[hi:,hi:]=a_ref[hi:,hi:]-dot3(r,r,((0,),(0,)))
            upd=dot3(r,w_ref[lo:hi,:hi],((0,),(0,)))
            if k==0: w_ref[hi:,:hi]=-upd
            else:
                w_ref[hi:,:lo]=w_ref[hi:,:lo]-upd[:,:lo]
                w_ref[hi:,lo:hi]=-upd[:,lo:]
    wh, wl = split(w_ref[...])
    left = left_ref[...]
    nt = lambda p, q: lax.dot_general(p, q, (((1,), (1,)), ((), ())), preferred_element_type=F)
    ortho_ref[...] = nt(left, wh) + nt(left, wl)


def orthonormal(gram, left):
    return pl.pallas_call(
        chol_kernel,
        out_shape=jax.ShapeDtypeStruct(left.shape, F),
        in_specs=[pl.BlockSpec(memory_space=pltpu.VMEM)] * 2,
        out_specs=pl.BlockSpec(memory_space=pltpu.VMEM),
        scratch_shapes=[pltpu.VMEM((N, N), F), pltpu.VMEM((N, N), F)],
        compiler_params=pltpu.CompilerParams(vmem_limit_bytes=32 * 2**20),
        name="orthonormal",
    )(gram, left)


def exchange(x, axis):
    return lax.all_to_all(x, axis, 0, 0, tiled=True)


def scatter_sum(x, axis, dtype):
    count = lax.axis_size(axis)
    pieces = exchange(x.astype(dtype).reshape(count, -1, x.shape[-1]), axis)
    return jnp.sum(pieces.astype(F), axis=0)


def gather(x, axis):
    count = lax.axis_size(axis)
    return exchange(jnp.broadcast_to(x[None], (count, *x.shape)), axis).reshape(-1, x.shape[-1])


def body(weights, gradient, momentum, basis):
    blend = momentum[0] + gradient[0].astype(F)
    blend16 = blend.astype(B)
    share = scatter_sum(jnp.dot(blend16, basis[0].astype(B), preferred_element_type=F), TP, B)
    left = gather(share.astype(B), TP)
    nn = lambda p, q, dims: lax.dot_general(p, q, (dims, ((), ())), preferred_element_type=F)
    gram = gather(scatter_sum(nn(left, left, ((0,), (0,))), FSDP, F), FSDP)
    ortho = orthonormal(gram, left)
    ortho16 = ortho.astype(B)
    right_share = scatter_sum(nn(blend16, ortho16, ((0,), (0,))), FSDP, B)
    right = lax.all_gather(right_share.astype(B), FSDP, axis=0, tiled=True)
    right32 = right.astype(F)
    squares = gather(jnp.sum(right32 * right32, axis=0, keepdims=True), TP)
    scale = lax.rsqrt(jnp.sum(squares, axis=0) / COLS + 1e-06)
    moment_new = blend - 0.05 * nn(ortho16, right, ((1,), (1,)))
    basis_new = right32 * scale
    update = nn((ortho * scale).astype(B), right, ((1,), (1,)))
    weight_new = (weights[0].astype(F) - 0.3 * update).astype(B)
    other = lax.ppermute(weight_new, "r", [(0, 1), (1, 0)])
    first = lax.axis_index("r") == 0
    both = jnp.where(first, jnp.stack([weight_new, other]), jnp.stack([other, weight_new]))
    return weight_new[None], moment_new[None], basis_new[None], both


def solution(mesh):
    finer = Mesh(mesh.devices.reshape(4, 2, 2, 8, 2), ("y", "c", "x", "z", "r"))
    split_specs = P("r", FSDP, TP)
    basis_spec = P("r", TP, None)
    return jax.shard_map(
        body,
        mesh=finer,
        in_specs=(split_specs, split_specs, split_specs, basis_spec),
        out_specs=(split_specs, split_specs, basis_spec, P(None, FSDP, TP)),
        check_vma=False,
    )
```

```python
import jax
import jax.numpy as jnp
from jax import lax
from jax.experimental import pallas as pl
from jax.experimental.pallas import tpu as pltpu
from jax.sharding import Mesh
from jax.sharding import PartitionSpec as P

COLS = 14336
TP = ("x", "z")
FSDP = ("y", "c")
F = jnp.float32
B = jnp.bfloat16
N = 512
NB = 128
GRP = 8
GR = 96
RR = 112
VMEM = pl.BlockSpec(memory_space=pltpu.VMEM)
SMEM = pl.BlockSpec(memory_space=pltpu.SMEM)


def call(kernel, outs, scratch=(), smem=0, name=None):
    def run(*args):
        return pl.pallas_call(
            kernel,
            out_shape=[jax.ShapeDtypeStruct(s, d) for s, d in outs],
            in_specs=[SMEM] * smem + [VMEM] * (len(args) - smem),
            out_specs=[VMEM] * len(outs),
            scratch_shapes=list(scratch),
            compiler_params=pltpu.CompilerParams(vmem_limit_bytes=48 * 2**20),
            name=name,
        )(*args)

    return run


def dot(p, q, over):
    return lax.dot_general(p, q, (over, ((), ())), preferred_element_type=F)


NN, NT, TN = ((1,), (0,)), ((1,), (1,)), ((0,), (0,))


def halves(x):
    hi = x.astype(B)
    return hi, (x - hi.astype(F)).astype(B)


def dot3(a, b, over):
    ah, al = halves(a)
    bh, bl = halves(b)
    return dot(ah, bh, over) + (dot(ah, bl, over) + dot(al, bh, over))


def total(v):
    while len(v) > 1:
        v = [v[i] + v[i + 1] if i + 1 < len(v) else v[i] for i in range(0, len(v), 2)]
    return v[0]


def factor(rows, inv_rows):
    n, w, b = len(rows), rows[0].shape[1], GRP
    sub = lax.broadcasted_iota(jnp.int32, (8, w), 0)
    full = lambda v: jnp.broadcast_to(v, (8, w))
    for p in range(n):
        j = 8 * p
        cols = [full(rows[p][:, j + m : j + m + 1]) for m in range(b)]
        d = [[full(cols[m][i : i + 1, :]) for m in range(i + 1)] for i in range(b)]
        row = [full(rows[p][m : m + 1, :]) for m in range(b)]
        erow = [full(inv_rows[p][m : m + 1, :]) for m in range(b)]
        v = [[None] * b for _ in range(b)]
        low = [[None] * b for _ in range(b)]
        for i in range(b):
            rt = lax.rsqrt(d[i][i])
            for m in range(i + 1, b):
                low[m][i] = d[m][i] * rt
            for m in range(i + 1, b):
                for t in range(i + 1, m + 1):
                    d[m][t] = d[m][t] - low[m][i] * low[t][i]
            v[i][i] = rt
            for t in range(i):
                v[i][t] = -(rt * total([low[i][k] * v[k][t] for k in range(t, i)]))
        r = [total([v[i][m] * row[m] for m in range(i + 1)]) for i in range(b)]
        e = [total([v[i][m] * erow[m] for m in range(i + 1)]) for i in range(b)]
        z = [total([v[i][m] * r[i] for i in range(m, b)]) for m in range(b)]
        ze = [total([v[i][m] * e[i] for i in range(m, b)]) for m in range(b)]
        for q in range(p + 1, n):
            c = [full(rows[q][:, j + m : j + m + 1]) for m in range(b)]
            rows[q] = rows[q] - total([c[m] * z[m] for m in range(b)])
            inv_rows[q] = inv_rows[q] - total([c[m] * ze[m] for m in range(b)])
        y = e[0]
        for i in range(1, b):
            y = jnp.where(sub == i, e[i], y)
        inv_rows[p] = y
    return inv_rows


def inverse_factor(a_ref, w_ref):
    ri = lax.broadcasted_iota(jnp.int32, (8, NB), 0)
    ci = lax.broadcasted_iota(jnp.int32, (8, NB), 1)
    for lo in range(0, N, NB):
        hi = lo + NB
        rows = [a_ref[lo + 8 * p : lo + 8 * p + 8, lo:hi] for p in range(NB // 8)]
        inv = factor(rows, [(ci == ri + 8 * p).astype(F) for p in range(NB // 8)])
        wkk = jnp.concatenate(inv, axis=0)
        w_ref[lo:hi, lo:hi] = wkk
        if hi < N:
            w_ref[lo:hi, hi:] = jnp.zeros((NB, N - hi), F)
        if lo > 0:
            w_ref[lo:hi, :lo] = dot3(wkk, w_ref[lo:hi, :lo], NN)
        if hi < N:
            r = dot3(wkk, a_ref[lo:hi, hi:], NN)
            for s in range(hi, N, NB):
                a_ref[s : s + NB, s:] = a_ref[s : s + NB, s:] - dot3(r[:, s - hi : s - hi + NB], r[:, s - hi :], TN)
            upd = dot3(r, w_ref[lo:hi, :hi], TN)
            if lo > 0:
                w_ref[hi:, :lo] = w_ref[hi:, :lo] - upd[:, :lo]
            w_ref[hi:, lo:hi] = -upd[:, lo:]


def pieces_kernel(core, left_ref, blend_ref, keep_g, keep_r, send, right_scr, part):
    right_scr[...] = dot(blend_ref[...], left_ref[...], TN)
    for mine in (True, False):
        c = core[0] if mine else 1 - core[0]
        wide = left_ref[:, pl.ds(pl.multiple_of(c * 256, 256), 256)]
        narrow = left_ref[:, pl.ds(pl.multiple_of(c * 128, 128), 128)]
        part[:256, :] = dot(wide, wide, TN)
        part[256:, :] = dot(narrow, left_ref[:, 256:], TN)
        for y in range(4):
            g = part[y * GR : (y + 1) * GR, :]
            r = right_scr[pl.ds(pl.multiple_of((2 * y + c) * RR, 16), RR), :]
            if mine:
                keep_g[y] = g
                keep_r[y] = r
            else:
                gh, gl = halves(g)
                send[y, :RR, :] = r.astype(B)
                send[y, RR:, :256] = gh
                send[y, RR:, 256:] = gl


def join_kernel(line, keep_g, keep_r, got, own_g, own_r, one, two, three):
    for k, out in enumerate((None, one, two, three)):
        y = line[0] ^ k
        r = keep_r[y] + got[y, :RR, :].astype(F)
        g = keep_g[y] + (got[y, RR:, :256].astype(F) + got[y, RR:, 256:].astype(F))
        if out is None:
            own_g[...] = g
            own_r[...] = r
        else:
            gh, gl = halves(g)
            out[:RR, :] = r.astype(B)
            out[RR:, :256] = gh
            out[RR:, 256:] = gl


def sum_kernel(own_g, own_r, one, two, three, out):
    g, r = own_g[...], own_r[...]
    for got in (one, two, three):
        r = r + got[:RR, :].astype(F)
        g = g + (got[RR:, :256].astype(F) + got[RR:, 256:].astype(F))
    gh, gl = halves(g)
    out[:RR, :] = r.astype(B)
    out[RR:, :256] = gh
    out[RR:, 256:] = gl


def split_kernel(both, right):
    for f in range(8):
        right[f * RR : (f + 1) * RR, :] = both[f, :RR, :]


def solve_kernel(both, left, right_in, w16, ortho, right, squares, a, w):
    for f in range(8):
        y, c = divmod(f, 2)
        g = both[f, RR:, :256].astype(F) + both[f, RR:, 256:].astype(F)
        first = y * GR
        square = max(0, min(GR, 256 - first))
        if square:
            a[c * 256 + first : c * 256 + first + square, c * 256 : c * 256 + 256] = g[:square, :]
        if square < GR:
            at = c * 128 + first + square - 256
            a[at : at + GR - square, 256:] = g[square:, :]
    inverse_factor(a, w)
    wh, wl = halves(w[...])
    w16[...] = wh
    ortho[...] = (dot(left[...], wh, NT) + dot(left[...], wl, NT)).astype(B)
    r = dot(right_in[...], wh, NT) + dot(right_in[...], wl, NT)
    right[...] = r
    squares[...] = jnp.sum(r * r, axis=0, keepdims=True)


def own_kernel(blend, ortho, right, scale, moment, basis):
    r = right[...]
    basis[...] = r * scale[...]
    moment[...] = blend[...] - 0.05 * dot(ortho[...], r.astype(B), NT)


def weight_kernel(side, left0, w0, right0, scale0, weight0, left1, w1, right1, scale1, weight1, own, out):
    for k, refs in enumerate(((left0, w0, right0, scale0, weight0), (left1, w1, right1, scale1, weight1))):
        left, w, right, scale, weight = (ref[...] for ref in refs)
        o = (dot(left, w, NT) * scale).astype(B)
        r = dot(right, w, NT).astype(B)
        new = (weight.astype(F) - 0.3 * dot(o, r, NT)).astype(B)
        if k == 0:
            own[...] = new
        out[side[0] if k == 0 else 1 - side[0]] = new


def exchange(x, axis):
    return lax.all_to_all(x, axis, 0, 0, tiled=True)


def gather(x, axis):
    count = lax.axis_size(axis)
    return exchange(jnp.broadcast_to(x[None], (count, *x.shape)), axis).reshape(-1, x.shape[-1])


def swap(x, axis, bit=1):
    return lax.ppermute(x, axis, [(i, i ^ bit) for i in range(lax.axis_size(axis))])


def body(weights, gradient, momentum, basis):
    index = lambda axis: lax.axis_index(axis).astype(jnp.int32).reshape(1)
    blend = momentum[0] + gradient[0].astype(F)
    blend16 = blend.astype(B)
    part = dot(blend16, basis[0].astype(B), NN).astype(B).reshape(16, -1, N)
    share = jnp.sum(exchange(part, TP).astype(F), axis=0).astype(B)
    left = gather(share, TP)

    keep_g, keep_r, send = call(
        pieces_kernel,
        [((4, GR, 256), F), ((4, RR, N), F), ((4, RR + GR, N), B)],
        [pltpu.VMEM((8 * RR, N), F), pltpu.VMEM((384, 256), F)],
        smem=1,
        name="pieces",
    )(index("c"), left, blend16)
    got = swap(send, "c")
    left_o = swap(left, "r")
    own_g, own_r, *outs = call(
        join_kernel,
        [((GR, 256), F), ((RR, N), F)] + [((RR + GR, N), B)] * 3,
        smem=1,
        name="join",
    )(index("y"), keep_g, keep_r, got)
    arrived = [swap(x, "y", k + 1) for k, x in enumerate(outs)]
    (piece,) = call(sum_kernel, [((RR + GR, N), B)], name="sum")(own_g, own_r, *arrived)
    both = lax.all_gather(piece, FSDP, axis=0, tiled=False)
    (raw,) = call(split_kernel, [((8 * RR, N), B)], name="split")(both)
    raw_o = swap(raw, "r")
    weight, _ = lax.optimization_barrier((weights[0], left))
    weight_o = swap(weight, "r")

    w16, ortho, right, squares = call(
        solve_kernel,
        [((N, N), B), ((N, N), B), ((8 * RR, N), F), ((1, N), F)],
        [pltpu.VMEM((N, N), F), pltpu.VMEM((N, N), F)],
        name="solve",
    )(both, left, raw)
    w16_o = swap(w16, "r")
    scale = lax.rsqrt(jnp.sum(gather(squares, TP), axis=0, keepdims=True) / COLS + 1e-06)
    scale_o = swap(scale, "r")
    moment_new, basis_new = call(own_kernel, [(blend.shape, F), (right.shape, F)], name="own")(
        blend, ortho, right, scale
    )
    weight_new, rollout = call(
        weight_kernel, [(weight.shape, B), ((2, *weight.shape), B)], smem=1, name="weights"
    )(index("r"), left, w16, raw, scale, weights[0], left_o, w16_o, raw_o, scale_o, weight_o)
    return weight_new[None], moment_new[None], basis_new[None], rollout


def solution(mesh):
    finer = Mesh(mesh.devices.reshape(4, 2, 2, 8, 2), ("y", "c", "x", "z", "r"))
    split_specs = P("r", FSDP, TP)
    basis_spec = P("r", TP, None)
    return jax.shard_map(
        body,
        mesh=finer,
        in_specs=(split_specs, split_specs, split_specs, basis_spec),
        out_specs=(split_specs, split_specs, basis_spec, P(None, FSDP, TP)),
        check_vma=False,
    )
```

```python
import jax
import jax.numpy as jnp
from jax import lax
from jax.experimental import pallas as pl
from jax.experimental.pallas import tpu as pltpu
from jax.sharding import Mesh
from jax.sharding import PartitionSpec as P

COLS = 14336
TP = ("x", "z")
FSDP = ("y", "c")
F = jnp.float32
B = jnp.bfloat16
N = 512
NB = 128
GRP = 8
GR = 96
RR = 112
VMEM = pl.BlockSpec(memory_space=pltpu.VMEM)
SMEM = pl.BlockSpec(memory_space=pltpu.SMEM)


def call(kernel, outs, scratch=(), smem=0, name=None, mib=12):
    def run(*args):
        return pl.pallas_call(
            kernel,
            out_shape=[jax.ShapeDtypeStruct(s, d) for s, d in outs],
            in_specs=[SMEM] * smem + [VMEM] * (len(args) - smem),
            out_specs=[VMEM] * len(outs),
            scratch_shapes=list(scratch),
            compiler_params=pltpu.CompilerParams(vmem_limit_bytes=mib * 2**20),
            name=name,
        )(*args)

    return run


def dot(p, q, over):
    return lax.dot_general(p, q, (over, ((), ())), preferred_element_type=F)


NN, NT, TN = ((1,), (0,)), ((1,), (1,)), ((0,), (0,))


def halves(x):
    hi = x.astype(B)
    return hi, (x - hi.astype(F)).astype(B)


def dot3(a, b, over):
    ah, al = halves(a)
    bh, bl = halves(b)
    return dot(ah, bh, over) + (dot(ah, bl, over) + dot(al, bh, over))


def total(v):
    while len(v) > 1:
        v = [v[i] + v[i + 1] if i + 1 < len(v) else v[i] for i in range(0, len(v), 2)]
    return v[0]


def factor(rows, inv_rows):
    n, w, b = len(rows), rows[0].shape[1], GRP
    sub = lax.broadcasted_iota(jnp.int32, (8, w), 0)
    full = lambda v: jnp.broadcast_to(v, (8, w))
    for p in range(n):
        j = 8 * p
        cols = [full(rows[p][:, j + m : j + m + 1]) for m in range(b)]
        d = [[full(cols[m][i : i + 1, :]) for m in range(i + 1)] for i in range(b)]
        row = [full(rows[p][m : m + 1, :]) for m in range(b)]
        erow = [full(inv_rows[p][m : m + 1, :]) for m in range(b)]
        v = [[None] * b for _ in range(b)]
        low = [[None] * b for _ in range(b)]
        for i in range(b):
            rt = lax.rsqrt(d[i][i])
            for m in range(i + 1, b):
                low[m][i] = d[m][i] * rt
            for m in range(i + 1, b):
                for t in range(i + 1, m + 1):
                    d[m][t] = d[m][t] - low[m][i] * low[t][i]
            v[i][i] = rt
            for t in range(i):
                v[i][t] = -(rt * total([low[i][k] * v[k][t] for k in range(t, i)]))
        r = [total([v[i][m] * row[m] for m in range(i + 1)]) for i in range(b)]
        e = [total([v[i][m] * erow[m] for m in range(i + 1)]) for i in range(b)]
        z = [total([v[i][m] * r[i] for i in range(m, b)]) for m in range(b)]
        ze = [total([v[i][m] * e[i] for i in range(m, b)]) for m in range(b)]
        for q in range(p + 1, n):
            c = [full(rows[q][:, j + m : j + m + 1]) for m in range(b)]
            rows[q] = rows[q] - total([c[m] * z[m] for m in range(b)])
            inv_rows[q] = inv_rows[q] - total([c[m] * ze[m] for m in range(b)])
        y = e[0]
        for i in range(1, b):
            y = jnp.where(sub == i, e[i], y)
        inv_rows[p] = y
    return inv_rows


def inverse_factor(a_ref, w_ref):
    ri = lax.broadcasted_iota(jnp.int32, (8, NB), 0)
    ci = lax.broadcasted_iota(jnp.int32, (8, NB), 1)
    for lo in range(0, N, NB):
        hi = lo + NB
        rows = [a_ref[lo + 8 * p : lo + 8 * p + 8, lo:hi] for p in range(NB // 8)]
        inv = factor(rows, [(ci == ri + 8 * p).astype(F) for p in range(NB // 8)])
        wkk = jnp.concatenate(inv, axis=0)
        w_ref[lo:hi, lo:hi] = wkk
        if hi < N:
            w_ref[lo:hi, hi:] = jnp.zeros((NB, N - hi), F)
        if lo > 0:
            w_ref[lo:hi, :lo] = dot3(wkk, w_ref[lo:hi, :lo], NN)
        if hi < N:
            r = dot3(wkk, a_ref[lo:hi, hi:], NN)
            for s in range(hi, N, NB):
                a_ref[s : s + NB, s:] = a_ref[s : s + NB, s:] - dot3(r[:, s - hi : s - hi + NB], r[:, s - hi :], TN)
            upd = dot3(r, w_ref[lo:hi, :hi], TN)
            if lo > 0:
                w_ref[hi:, :lo] = w_ref[hi:, :lo] - upd[:, :lo]
            w_ref[hi:, lo:hi] = -upd[:, lo:]


def pieces_kernel(core, left_ref, blend_ref, keep_g, keep_r, send, right_scr, part):
    right_scr[...] = dot(blend_ref[...], left_ref[...], TN)
    for mine in (True, False):
        c = core[0] if mine else 1 - core[0]
        wide = left_ref[:, pl.ds(pl.multiple_of(c * 256, 256), 256)]
        narrow = left_ref[:, pl.ds(pl.multiple_of(c * 128, 128), 128)]
        part[:256, :] = dot(wide, wide, TN)
        part[256:, :] = dot(narrow, left_ref[:, 256:], TN)
        for y in range(4):
            g = part[y * GR : (y + 1) * GR, :]
            r = right_scr[pl.ds(pl.multiple_of((2 * y + c) * RR, 16), RR), :]
            if mine:
                keep_g[y] = g
                keep_r[y] = r
            else:
                gh, gl = halves(g)
                send[y, :RR, :] = r.astype(B)
                send[y, RR:, :256] = gh
                send[y, RR:, 256:] = gl


def join_kernel(line, keep_g, keep_r, got, own_g, own_r, one, two, three):
    for k, out in enumerate((None, one, two, three)):
        y = line[0] ^ k
        r = keep_r[y] + got[y, :RR, :].astype(F)
        g = keep_g[y] + (got[y, RR:, :256].astype(F) + got[y, RR:, 256:].astype(F))
        if out is None:
            own_g[...] = g
            own_r[...] = r
        else:
            gh, gl = halves(g)
            out[:RR, :] = r.astype(B)
            out[RR:, :256] = gh
            out[RR:, 256:] = gl


def sum_kernel(own_g, own_r, one, two, three, piece, share):
    g, r = own_g[...], own_r[...]
    for got in (one, two, three):
        r = r + got[:RR, :].astype(F)
        g = g + (got[RR:, :256].astype(F) + got[RR:, 256:].astype(F))
    gh, gl = halves(g)
    share[...] = r.astype(B)
    piece[:, :256] = gh
    piece[:, 256:] = gl


def solve_kernel(both, left, w16, w_low, ortho, a, w):
    for f in range(8):
        y, c = divmod(f, 2)
        g = both[f * GR : (f + 1) * GR, :256].astype(F) + both[f * GR : (f + 1) * GR, 256:].astype(F)
        first = y * GR
        square = max(0, min(GR, 256 - first))
        if square:
            a[c * 256 + first : c * 256 + first + square, c * 256 : c * 256 + 256] = g[:square, :]
        if square < GR:
            at = c * 128 + first + square - 256
            a[at : at + GR - square, 256:] = g[square:, :]
    inverse_factor(a, w)
    wh, wl = halves(w[...])
    w16[...] = wh
    w_low[...] = wl
    ortho[...] = (dot(left[...], wh, NT) + dot(left[...], wl, NT)).astype(B)


def rows_from(place, k, other_core):
    y, c = place[0] ^ k, place[1]
    return pl.ds(pl.multiple_of((2 * y + (1 - c if other_core else c)) * RR, 16), RR)


def right_kernel(place, w16, w_low, s0, s1, s2, s3, right, squares):
    acc = jnp.zeros((1, N), F)
    for k, s in enumerate((s0, s1, s2, s3)):
        for slot in range(2):
            r = dot(s[slot], w16[...], NT) + dot(s[slot], w_low[...], NT)
            right[rows_from(place, k, slot == 1), :] = r
            acc = acc + jnp.sum(r * r, axis=0, keepdims=True)
    squares[...] = acc


def own_kernel(blend, ortho, right, scale, moment, basis):
    r = right[...]
    basis[...] = r * scale[...]
    moment[...] = blend[...] - 0.05 * dot(ortho[...], r.astype(B), NT)


def weight_kernel(place, s0, s1, s2, s3, left0, w0, scale0, weight0, left1, w1, scale1, weight1, own, out, r_ref):
    for half, refs in enumerate(((left0, w0, scale0, weight0), (left1, w1, scale1, weight1))):
        left, w, scale, weight = (ref[...] for ref in refs)
        o = (dot(left, w, NT) * scale).astype(B)
        for k, s in enumerate((s0, s1, s2, s3)):
            for slot in range(2):
                r_ref[rows_from(place, k, slot == 1), :] = dot(s[2 * half + slot], w, NT).astype(B)
        new = (weight.astype(F) - 0.3 * dot(o, r_ref[...], NT)).astype(B)
        if half == 0:
            own[...] = new
        out[place[2] if half == 0 else 1 - place[2]] = new


def exchange(x, axis):
    return lax.all_to_all(x, axis, 0, 0, tiled=True)


def gather(x, axis):
    count = lax.axis_size(axis)
    return exchange(jnp.broadcast_to(x[None], (count, *x.shape)), axis).reshape(-1, x.shape[-1])


def swap(x, axis, bit=1):
    return lax.ppermute(x, axis, [(i, i ^ bit) for i in range(lax.axis_size(axis))])


def body(weights, gradient, momentum, basis):
    index = lambda axis: lax.axis_index(axis).astype(jnp.int32).reshape(1)
    blend = momentum[0] + gradient[0].astype(F)
    blend16 = blend.astype(B)
    part = dot(blend16, basis[0].astype(B), NN).astype(B).reshape(16, -1, N)
    share = jnp.sum(exchange(part, TP).astype(F), axis=0).astype(B)
    left = gather(share, TP)

    keep_g, keep_r, send = call(
        pieces_kernel,
        [((4, GR, 256), F), ((4, RR, N), F), ((4, RR + GR, N), B)],
        [pltpu.VMEM((8 * RR, N), F), pltpu.VMEM((384, 256), F)],
        smem=1,
        name="pieces",
    )(index("c"), left, blend16)
    got = swap(send, "c")
    left_o = swap(left, "r")
    own_g, own_r, *outs = call(
        join_kernel,
        [((GR, 256), F), ((RR, N), F)] + [((RR + GR, N), B)] * 3,
        smem=1,
        name="join",
    )(index("y"), keep_g, keep_r, got)
    arrived = [swap(x, "y", k + 1) for k, x in enumerate(outs)]
    piece, share = call(sum_kernel, [((GR, N), B), ((RR, N), B)], name="sum")(own_g, own_r, *arrived)
    from_core = swap(share, "c")
    from_other = swap(share, "r")
    from_both = lax.ppermute(share, ("c", "r"), [(i, 3 - i) for i in range(4)])
    gram = lax.all_gather(piece, FSDP, axis=0, tiled=True)
    stack = [jnp.stack([share, from_core, from_other, from_both])]
    stack += [swap(stack[0], "y", k) for k in (1, 2, 3)]
    weight, _ = lax.optimization_barrier((weights[0], left))
    weight_o = swap(weight, "r")

    w16, w_low, ortho = call(
        solve_kernel,
        [((N, N), B)] * 3,
        [pltpu.VMEM((N, N), F), pltpu.VMEM((N, N), F)],
        name="solve",
    )(gram, left)
    w16_o = swap(w16, "r")
    place = jnp.concatenate([index("y"), index("c"), index("r")])
    right, squares = call(right_kernel, [((8 * RR, N), F), ((1, N), F)], smem=1, name="right")(
        place, w16, w_low, *stack
    )
    scale = lax.rsqrt(jnp.sum(gather(squares, TP), axis=0, keepdims=True) / COLS + 1e-06)
    scale_o = swap(scale, "r")
    moment_new, basis_new = call(own_kernel, [(blend.shape, F), (right.shape, F)], name="own")(
        blend, ortho, right, scale
    )
    weight_new, rollout = call(
        weight_kernel,
        [(weight.shape, B), ((2, *weight.shape), B)],
        [pltpu.VMEM((8 * RR, N), B)],
        smem=1,
        name="weights",
    )(place, *stack, left, w16, scale, weights[0], left_o, w16_o, scale_o, weight_o)
    return weight_new[None], moment_new[None], basis_new[None], rollout


def solution(mesh):
    finer = Mesh(mesh.devices.reshape(4, 2, 2, 8, 2), ("y", "c", "x", "z", "r"))
    split_specs = P("r", FSDP, TP)
    basis_spec = P("r", TP, None)
    return jax.shard_map(
        body,
        mesh=finer,
        in_specs=(split_specs, split_specs, split_specs, basis_spec),
        out_specs=(split_specs, split_specs, basis_spec, P(None, FSDP, TP)),
        check_vma=False,
    )
```

```python
import jax
import jax.numpy as jnp
from jax import lax
from jax.experimental import pallas as pl
from jax.experimental.pallas import tpu as pltpu
from jax.sharding import Mesh
from jax.sharding import PartitionSpec as P

COLS = 14336
TP = ("x", "z")
FSDP = ("y", "c")
F = jnp.float32
B = jnp.bfloat16
N = 512
NB = 128
GRP = 8
GR = 96
RR = 112
VMEM = pl.BlockSpec(memory_space=pltpu.VMEM)
SMEM = pl.BlockSpec(memory_space=pltpu.SMEM)


def call(kernel, outs, scratch=(), smem=0, name=None, mib=12, out_spec=VMEM):
    def run(*args):
        return pl.pallas_call(
            kernel,
            out_shape=[jax.ShapeDtypeStruct(s, d) for s, d in outs],
            in_specs=[SMEM] * smem + [VMEM] * (len(args) - smem),
            out_specs=[out_spec] * len(outs),
            scratch_shapes=list(scratch),
            compiler_params=pltpu.CompilerParams(vmem_limit_bytes=mib * 2**20),
            name=name,
        )(*args)

    return run


def dot(p, q, over):
    return lax.dot_general(p, q, (over, ((), ())), preferred_element_type=F)


NN, NT, TN = ((1,), (0,)), ((1,), (1,)), ((0,), (0,))


def halves(x):
    hi = x.astype(B)
    return hi, (x - hi.astype(F)).astype(B)


def dot3(a, b, over):
    ah, al = halves(a)
    bh, bl = halves(b)
    return dot(ah, bh, over) + (dot(ah, bl, over) + dot(al, bh, over))


def total(v):
    while len(v) > 1:
        v = [v[i] + v[i + 1] if i + 1 < len(v) else v[i] for i in range(0, len(v), 2)]
    return v[0]


def factor(rows, inv_rows):
    n, w, b = len(rows), rows[0].shape[1], GRP
    sub = lax.broadcasted_iota(jnp.int32, (8, w), 0)
    full = lambda v: jnp.broadcast_to(v, (8, w))
    for p in range(n):
        j = 8 * p
        cols = [full(rows[p][:, j + m : j + m + 1]) for m in range(b)]
        d = [[full(cols[m][i : i + 1, :]) for m in range(i + 1)] for i in range(b)]
        row = [full(rows[p][m : m + 1, :]) for m in range(b)]
        erow = [full(inv_rows[p][m : m + 1, :]) for m in range(b)]
        v = [[None] * b for _ in range(b)]
        low = [[None] * b for _ in range(b)]
        for i in range(b):
            rt = lax.rsqrt(d[i][i])
            for m in range(i + 1, b):
                low[m][i] = d[m][i] * rt
            for m in range(i + 1, b):
                for t in range(i + 1, m + 1):
                    d[m][t] = d[m][t] - low[m][i] * low[t][i]
            v[i][i] = rt
            for t in range(i):
                v[i][t] = -(rt * total([low[i][k] * v[k][t] for k in range(t, i)]))
        r = [total([v[i][m] * row[m] for m in range(i + 1)]) for i in range(b)]
        e = [total([v[i][m] * erow[m] for m in range(i + 1)]) for i in range(b)]
        z = [total([v[i][m] * r[i] for i in range(m, b)]) for m in range(b)]
        ze = [total([v[i][m] * e[i] for i in range(m, b)]) for m in range(b)]
        for q in range(p + 1, n):
            c = [full(rows[q][:, j + m : j + m + 1]) for m in range(b)]
            rows[q] = rows[q] - total([c[m] * z[m] for m in range(b)])
            inv_rows[q] = inv_rows[q] - total([c[m] * ze[m] for m in range(b)])
        y = e[0]
        for i in range(1, b):
            y = jnp.where(sub == i, e[i], y)
        inv_rows[p] = y
    return inv_rows


def inverse_factor(a_ref, w_ref):
    ri = lax.broadcasted_iota(jnp.int32, (8, NB), 0)
    ci = lax.broadcasted_iota(jnp.int32, (8, NB), 1)
    for lo in range(0, N, NB):
        hi = lo + NB
        rows = [a_ref[lo + 8 * p : lo + 8 * p + 8, lo:hi] for p in range(NB // 8)]
        inv = factor(rows, [(ci == ri + 8 * p).astype(F) for p in range(NB // 8)])
        wkk = jnp.concatenate(inv, axis=0)
        w_ref[lo:hi, lo:hi] = wkk
        if hi < N:
            w_ref[lo:hi, hi:] = jnp.zeros((NB, N - hi), F)
        if lo > 0:
            w_ref[lo:hi, :lo] = dot3(wkk, w_ref[lo:hi, :lo], NN)
        if hi < N:
            r = dot3(wkk, a_ref[lo:hi, hi:], NN)
            for s in range(hi, N, NB):
                a_ref[s : s + NB, s:] = a_ref[s : s + NB, s:] - dot3(r[:, s - hi : s - hi + NB], r[:, s - hi :], TN)
            upd = dot3(r, w_ref[lo:hi, :hi], TN)
            if lo > 0:
                w_ref[hi:, :lo] = w_ref[hi:, :lo] - upd[:, :lo]
            w_ref[hi:, lo:hi] = -upd[:, lo:]


def spread_kernel(pieces, out):
    share = pieces[0].astype(F)
    for k in range(1, pieces.shape[0]):
        share = share + pieces[k].astype(F)
    share = share.astype(B)
    for k in range(out.shape[0]):
        out[k] = share


def pieces_kernel(place, left_ref, blend_ref, keep_g, keep_r, send, right_scr, part):
    right_scr[...] = dot(blend_ref[...], left_ref[...], TN)
    for mine in (True, False):
        c = place[1] if mine else 1 - place[1]
        wide = left_ref[:, pl.ds(pl.multiple_of(c * 256, 256), 256)]
        narrow = left_ref[:, pl.ds(pl.multiple_of(c * 128, 128), 128)]
        part[:256, :] = dot(wide, wide, TN)
        part[256:, :] = dot(narrow, left_ref[:, 256:], TN)
        for y in range(4):
            g = part[y * GR : (y + 1) * GR, :]
            r = right_scr[pl.ds(pl.multiple_of((2 * y + c) * RR, 16), RR), :]
            if mine:
                keep_g[y] = g
                keep_r[y] = r
            else:
                packed(send.at[y], g, r)


def packed(out, g, r):
    gh, gl = halves(g)
    out[:RR, :] = r.astype(B)
    out[RR:, :256] = gh
    out[RR:, 256:] = gl


def gram_of(ref):
    return ref[RR:, :256].astype(F) + ref[RR:, 256:].astype(F)


def join_kernel(place, keep_g, keep_r, got, own_g, own_r, one, two, three):
    for k, out in enumerate((None, one, two, three)):
        y = place[0] ^ k
        r = keep_r[y] + got[y, :RR, :].astype(F)
        g = keep_g[y] + gram_of(got.at[y])
        if out is None:
            own_g[...] = g
            own_r[...] = r
        else:
            packed(out, g, r)


def sum_kernel(own_g, own_r, one, two, three, out):
    g, r = own_g[...], own_r[...]
    for got in (one, two, three):
        r = r + got[:RR, :].astype(F)
        g = g + gram_of(got)
    packed(out, g, r)


def line_kernel(place, own, one, two, three, out):
    for k, got in enumerate((own, one, two, three)):
        out[place[0] ^ k] = got[...]


def rows_kernel(place, own, got, right):
    for y in range(4):
        for c, part in ((place[1], own), (1 - place[1], got)):
            right[pl.ds(pl.multiple_of((2 * y + c) * RR, 16), RR), :] = part[y, :RR, :]


def solve_kernel(place, own, got, left, right_in, w16, ortho, right, squares, a, w):
    for y in range(4):
        first = y * GR
        square = max(0, min(GR, 256 - first))
        for c, part in ((place[1], own), (1 - place[1], got)):
            g = gram_of(part.at[y])
            if square:
                rows = pl.ds(pl.multiple_of(c * 256 + first, 32), square)
                a[rows, pl.ds(pl.multiple_of(c * 256, 256), 256)] = g[:square, :]
            if square < GR:
                rows = pl.ds(pl.multiple_of(c * 128 + first + square - 256, 32), GR - square)
                a[rows, 256:] = g[square:, :]
    inverse_factor(a, w)
    wh, wl = halves(w[...])
    w16[...] = wh
    ortho[...] = (dot(left[...], wh, NT) + dot(left[...], wl, NT)).astype(B)
    r = dot(right_in[...], wh, NT) + dot(right_in[...], wl, NT)
    right[...] = r
    squares[...] = jnp.sum(r * r, axis=0, keepdims=True)


def last_kernel(
    place, sums, momentum, gradient, ortho, right, left0, w0, right0, weight0, left1, w1, right1, weight1,
    out_weight, out_moment, out_basis, out_rollout, weight, moment, basis, sems,
):
    scales = lax.rsqrt(jnp.sum(sums[...], axis=0) / COLS + 1e-06)
    first = place[2] == 0
    scale = [jnp.where(first, scales[0:1], scales[1:2]), jnp.where(first, scales[1:2], scales[0:1])]
    basis[...] = right[...] * scale[0]
    copies = [pltpu.make_async_copy(basis, out_basis, sems.at[0])]
    copies[-1].start()
    blend = momentum[...] + gradient[...].astype(F)
    moment[...] = blend - 0.05 * dot(ortho[...], right[...].astype(B), NT)
    copies.append(pltpu.make_async_copy(moment, out_moment, sems.at[1]))
    copies[-1].start()
    for half, refs in enumerate(((left0, w0, right0, weight0), (left1, w1, right1, weight1))):
        left, w, raw, old = (ref[...] for ref in refs)
        o = (dot(left, w, NT) * scale[half]).astype(B)
        r = dot(raw, w, NT).astype(B)
        weight[half] = (old.astype(F) - 0.3 * dot(o, r, NT)).astype(B)
        side = place[2] if half == 0 else 1 - place[2]
        copies.append(pltpu.make_async_copy(weight.at[half], out_rollout.at[side], sems.at[2 + half]))
        copies[-1].start()
        if half == 0:
            copies.append(pltpu.make_async_copy(weight.at[0], out_weight, sems.at[4]))
            copies[-1].start()
    for copy in copies:
        copy.wait()


def exchange(x, axis):
    return lax.all_to_all(x, axis, 0, 0, tiled=True)


def swap(x, axis, bit=1):
    return lax.ppermute(x, axis, [(i, i ^ bit) for i in range(lax.axis_size(axis))])


def body(weights, gradient, momentum, basis):
    place = jnp.stack([lax.axis_index(axis) for axis in ("y", "c", "r")]).astype(jnp.int32)
    place, basis = lax.optimization_barrier((place, basis))
    momentum, gradient = momentum[0], gradient[0]
    blend16 = (momentum + gradient.astype(F)).astype(B)
    part = dot(blend16, basis[0].astype(B), NN).astype(B).reshape(16, -1, N)
    (copies,) = call(spread_kernel, [(part.shape, B)], name="spread")(exchange(part, TP))
    left = exchange(copies, TP).reshape(-1, N)

    keep_g, keep_r, send = call(
        pieces_kernel,
        [((4, GR, 256), F), ((4, RR, N), F), ((4, RR + GR, N), B)],
        [pltpu.VMEM((8 * RR, N), F), pltpu.VMEM((384, 256), F)],
        smem=1,
        name="pieces",
    )(place, left, blend16)
    got = swap(send, "c")
    own_g, own_r, *outs = call(
        join_kernel,
        [((GR, 256), F), ((RR, N), F)] + [((RR + GR, N), B)] * 3,
        smem=1,
        name="join",
    )(place, keep_g, keep_r, got)
    arrived = [swap(x, "y", k + 1) for k, x in enumerate(outs)]
    (piece,) = call(sum_kernel, [((RR + GR, N), B)], name="sum")(own_g, own_r, *arrived)
    (line,) = call(line_kernel, [((4, RR + GR, N), B)], smem=1, name="line")(
        place, piece, *[swap(piece, "y", k) for k in (1, 2, 3)]
    )
    other_core = swap(line, "c")
    (raw,) = call(rows_kernel, [((8 * RR, N), B)], smem=1, name="rows")(place, line, other_core)
    raw_o = swap(raw, "r")
    left_o = swap(left, "r")
    weight, _ = lax.optimization_barrier((weights[0], left))
    weight_o = swap(weight, "r")

    w16, ortho, right, squares = call(
        solve_kernel,
        [((N, N), B), ((N, N), B), ((8 * RR, N), F), ((1, N), F)],
        [pltpu.VMEM((N, N), F), pltpu.VMEM((N, N), F)],
        smem=1,
        name="solve",
    )(place, line, other_core, left, raw)
    w16_o = swap(w16, "r")
    sums = exchange(jnp.broadcast_to(squares[None], (32, 1, N)), ("x", "z", "r")).reshape(16, 2, N)
    wide, tall = weight.shape, right.shape
    weight_new, moment_new, basis_new, rollout = call(
        last_kernel,
        [(wide, B), (wide, F), (tall, F), ((2, *wide), B)],
        [pltpu.VMEM((2, *wide), B), pltpu.VMEM(wide, F), pltpu.VMEM(tall, F), pltpu.SemaphoreType.DMA((5,))],
        smem=1,
        name="last",
        mib=24,
        out_spec=pl.BlockSpec(memory_space=pl.ANY),
    )(place, sums, momentum, gradient, ortho, right, left, w16, raw, weights[0], left_o, w16_o, raw_o, weight_o)
    return weight_new[None], moment_new[None], basis_new[None], rollout


def solution(mesh):
    finer = Mesh(mesh.devices.reshape(4, 2, 2, 8, 2), ("y", "c", "x", "z", "r"))
    split_specs = P("r", FSDP, TP)
    basis_spec = P("r", TP, None)
    return jax.shard_map(
        body,
        mesh=finer,
        in_specs=(split_specs, split_specs, split_specs, basis_spec),
        out_specs=(split_specs, split_specs, basis_spec, P(None, FSDP, TP)),
        check_vma=False,
    )
```

```python
import jax
import jax.numpy as jnp
from jax import lax
from jax.experimental import pallas as pl
from jax.experimental.pallas import tpu as pltpu
from jax.sharding import Mesh
from jax.sharding import PartitionSpec as P

COLS = 14336
TP = ("x", "z")
FSDP = ("y", "c")
F = jnp.float32
B = jnp.bfloat16
N = 512
NB = 128
GRP = 8
GR = 96
RR = 112
VMEM = pl.BlockSpec(memory_space=pltpu.VMEM)
SMEM = pl.BlockSpec(memory_space=pltpu.SMEM)


def call(kernel, outs, scratch=(), smem=0, name=None, mib=12, out_spec=VMEM):
    def run(*args):
        return pl.pallas_call(
            kernel,
            out_shape=[jax.ShapeDtypeStruct(s, d) for s, d in outs],
            in_specs=[SMEM] * smem + [VMEM] * (len(args) - smem),
            out_specs=[out_spec] * len(outs),
            scratch_shapes=list(scratch),
            compiler_params=pltpu.CompilerParams(vmem_limit_bytes=mib * 2**20),
            name=name,
        )(*args)

    return run


def dot(p, q, over):
    return lax.dot_general(p, q, (over, ((), ())), preferred_element_type=F)


NN, NT, TN = ((1,), (0,)), ((1,), (1,)), ((0,), (0,))


def halves(x):
    hi = x.astype(B)
    return hi, (x - hi.astype(F)).astype(B)


def dot3(a, b, over):
    ah, al = halves(a)
    bh, bl = halves(b)
    return dot(ah, bh, over) + (dot(ah, bl, over) + dot(al, bh, over))


def total(v):
    while len(v) > 1:
        v = [v[i] + v[i + 1] if i + 1 < len(v) else v[i] for i in range(0, len(v), 2)]
    return v[0]


def factor(rows, inv_rows):
    n, w, b = len(rows), rows[0].shape[1], GRP
    sub = lax.broadcasted_iota(jnp.int32, (8, w), 0)
    full = lambda v: jnp.broadcast_to(v, (8, w))
    for p in range(n):
        j = 8 * p
        cols = [full(rows[p][:, j + m : j + m + 1]) for m in range(b)]
        d = [[full(cols[m][i : i + 1, :]) for m in range(i + 1)] for i in range(b)]
        row = [full(rows[p][m : m + 1, :]) for m in range(b)]
        erow = [full(inv_rows[p][m : m + 1, :]) for m in range(b)]
        v = [[None] * b for _ in range(b)]
        low = [[None] * b for _ in range(b)]
        for i in range(b):
            rt = lax.rsqrt(d[i][i])
            for m in range(i + 1, b):
                low[m][i] = d[m][i] * rt
            for m in range(i + 1, b):
                for t in range(i + 1, m + 1):
                    d[m][t] = d[m][t] - low[m][i] * low[t][i]
            v[i][i] = rt
            for t in range(i):
                v[i][t] = -(rt * total([low[i][k] * v[k][t] for k in range(t, i)]))
        r = [total([v[i][m] * row[m] for m in range(i + 1)]) for i in range(b)]
        e = [total([v[i][m] * erow[m] for m in range(i + 1)]) for i in range(b)]
        z = [total([v[i][m] * r[i] for i in range(m, b)]) for m in range(b)]
        ze = [total([v[i][m] * e[i] for i in range(m, b)]) for m in range(b)]
        for q in range(p + 1, n):
            c = [full(rows[q][:, j + m : j + m + 1]) for m in range(b)]
            rows[q] = rows[q] - total([c[m] * z[m] for m in range(b)])
            inv_rows[q] = inv_rows[q] - total([c[m] * ze[m] for m in range(b)])
        y = e[0]
        for i in range(1, b):
            y = jnp.where(sub == i, e[i], y)
        inv_rows[p] = y
    return inv_rows


def inverse_factor(a_ref, w_ref):
    ri = lax.broadcasted_iota(jnp.int32, (8, NB), 0)
    ci = lax.broadcasted_iota(jnp.int32, (8, NB), 1)
    for lo in range(0, N, NB):
        hi = lo + NB
        rows = [a_ref[lo + 8 * p : lo + 8 * p + 8, lo:hi] for p in range(NB // 8)]
        inv = factor(rows, [(ci == ri + 8 * p).astype(F) for p in range(NB // 8)])
        wkk = jnp.concatenate(inv, axis=0)
        w_ref[lo:hi, lo:hi] = wkk
        if hi < N:
            w_ref[lo:hi, hi:] = jnp.zeros((NB, N - hi), F)
        if lo > 0:
            w_ref[lo:hi, :lo] = dot3(wkk, w_ref[lo:hi, :lo], NN)
        if hi < N:
            r = dot3(wkk, a_ref[lo:hi, hi:], NN)
            for s in range(hi, N, NB):
                a_ref[s : s + NB, s:] = a_ref[s : s + NB, s:] - dot3(r[:, s - hi : s - hi + NB], r[:, s - hi :], TN)
            upd = dot3(r, w_ref[lo:hi, :hi], TN)
            if lo > 0:
                w_ref[hi:, :lo] = w_ref[hi:, :lo] - upd[:, :lo]
            w_ref[hi:, lo:hi] = -upd[:, lo:]


def spread_kernel(pieces, out):
    share = pieces[0].astype(F)
    for k in range(1, pieces.shape[0]):
        share = share + pieces[k].astype(F)
    share = share.astype(B)
    for k in range(out.shape[0]):
        out[k] = share


def pieces_kernel(place, left_ref, blend_ref, keep_g, keep_r, send, right_scr, part):
    right_scr[...] = dot(blend_ref[...], left_ref[...], TN)
    for mine in (True, False):
        c = place[1] if mine else 1 - place[1]
        wide = left_ref[:, pl.ds(pl.multiple_of(c * 256, 256), 256)]
        narrow = left_ref[:, pl.ds(pl.multiple_of(c * 128, 128), 128)]
        part[:256, :] = dot(wide, wide, TN)
        part[256:, :] = dot(narrow, left_ref[:, 256:], TN)
        for y in range(4):
            g = part[y * GR : (y + 1) * GR, :]
            r = right_scr[pl.ds(pl.multiple_of((2 * y + c) * RR, 16), RR), :]
            if mine:
                keep_g[y] = g
                keep_r[y] = r
            else:
                packed(send.at[y], g, r)


def packed(out, g, r):
    gh, gl = halves(g)
    out[:RR, :] = r.astype(B)
    out[RR:, :256] = gh
    out[RR:, 256:] = gl


def gram_of(ref):
    return ref[RR:, :256].astype(F) + ref[RR:, 256:].astype(F)


def join_kernel(place, keep_g, keep_r, got, own_g, own_r, one, two, three):
    for k, out in enumerate((None, one, two, three)):
        y = place[0] ^ k
        r = keep_r[y] + got[y, :RR, :].astype(F)
        g = keep_g[y] + gram_of(got.at[y])
        if out is None:
            own_g[...] = g
            own_r[...] = r
        else:
            packed(out, g, r)


def sum_kernel(own_g, own_r, one, two, three, out):
    g, r = own_g[...], own_r[...]
    for got in (one, two, three):
        r = r + got[:RR, :].astype(F)
        g = g + gram_of(got)
    packed(out, g, r)


def line_kernel(place, own, one, two, three, out):
    for k, got in enumerate((own, one, two, three)):
        out[place[0] ^ k] = got[...]


def rows_kernel(place, own, got, right):
    for y in range(4):
        for c, part in ((place[1], own), (1 - place[1], got)):
            right[pl.ds(pl.multiple_of((2 * y + c) * RR, 16), RR), :] = part[y, :RR, :]


def solve_kernel(place, own, got, left, right_in, w16, ortho, right, squares, a, w):
    for y in range(4):
        first = y * GR
        square = max(0, min(GR, 256 - first))
        for c, part in ((place[1], own), (1 - place[1], got)):
            g = gram_of(part.at[y])
            if square:
                rows = pl.ds(pl.multiple_of(c * 256 + first, 32), square)
                a[rows, pl.ds(pl.multiple_of(c * 256, 256), 256)] = g[:square, :]
            if square < GR:
                rows = pl.ds(pl.multiple_of(c * 128 + first + square - 256, 32), GR - square)
                a[rows, 256:] = g[square:, :]
    inverse_factor(a, w)
    wh, wl = halves(w[...])
    w16[:256, :] = wh[256:, :]
    w16[256:, :256] = wh[:128, :256]
    w16[256:, 256:] = wh[128:256, :256]
    ortho[...] = (dot(left[...], wh, NT) + dot(left[...], wl, NT)).astype(B)
    r = dot(right_in[...], wh, NT) + dot(right_in[...], wl, NT)
    right[...] = r
    squares[...] = jnp.sum(r * r, axis=0, keepdims=True)


def last_kernel(
    place, sums, momentum, gradient, ortho, right, left0, w0, right0, weight0, left1, w1, right1, weight1,
    out_weight, out_moment, out_basis, out_rollout, weight, moment, basis, w, sems,
):
    scales = []
    for side in range(2):
        squares = sums[side]
        for k in range(2 + side, 32, 2):
            squares = squares + sums[k]
        scales.append(lax.rsqrt(squares / COLS + 1e-06))
    first = place[2] == 0
    scale = [jnp.where(first, *scales), jnp.where(first, *scales[::-1])]
    basis[...] = right[...] * scale[0]
    copies = [pltpu.make_async_copy(basis, out_basis, sems.at[0])]
    copies[-1].start()
    blend = momentum[...] + gradient[...].astype(F)
    moment[...] = blend - 0.05 * dot(ortho[...], right[...].astype(B), NT)
    copies.append(pltpu.make_async_copy(moment, out_moment, sems.at[1]))
    copies[-1].start()
    for half, refs in enumerate(((left0, w0, right0, weight0), (left1, w1, right1, weight1))):
        left, packed_w, raw, old = refs
        w[256:, :] = packed_w[:256, :]
        w[:128, :256] = packed_w[256:, :256]
        w[128:256, :256] = packed_w[256:, 256:]
        w[:256, 256:] = jnp.zeros((256, 256), B)
        o = (dot(left[...], w[...], NT) * scale[half]).astype(B)
        r = dot(raw[...], w[...], NT).astype(B)
        weight[half] = (old[...].astype(F) - 0.3 * dot(o, r, NT)).astype(B)
        side = place[2] if half == 0 else 1 - place[2]
        copies.append(pltpu.make_async_copy(weight.at[half], out_rollout.at[side], sems.at[2 + half]))
        copies[-1].start()
        if half == 0:
            copies.append(pltpu.make_async_copy(weight.at[0], out_weight, sems.at[4]))
            copies[-1].start()
    for copy in copies:
        copy.wait()


def exchange(x, axis):
    return lax.all_to_all(x, axis, 0, 0, tiled=True)


def swap(x, axis, bit=1):
    return lax.ppermute(x, axis, [(i, i ^ bit) for i in range(lax.axis_size(axis))])


def body(weights, gradient, momentum, basis):
    place = jnp.stack([lax.axis_index(axis) for axis in ("y", "c", "r")]).astype(jnp.int32)
    place, basis = lax.optimization_barrier((place, basis))
    momentum, gradient = momentum[0], gradient[0]
    blend16 = (momentum + gradient.astype(F)).astype(B)
    part = dot(blend16, basis[0].astype(B), NN).astype(B).reshape(16, -1, N)
    blend16, part = lax.optimization_barrier((blend16, part))
    (copies,) = call(spread_kernel, [(part.shape, B)], name="spread")(exchange(part, TP))
    left = exchange(copies, TP).reshape(-1, N)

    keep_g, keep_r, send = call(
        pieces_kernel,
        [((4, GR, 256), F), ((4, RR, N), F), ((4, RR + GR, N), B)],
        [pltpu.VMEM((8 * RR, N), F), pltpu.VMEM((384, 256), F)],
        smem=1,
        name="pieces",
    )(place, left, blend16)
    got = swap(send, "c")
    left_o = swap(left, "r")
    weight, _ = lax.optimization_barrier((weights[0], left))
    weight_o = swap(weight, "r")
    own_g, own_r, *outs = call(
        join_kernel,
        [((GR, 256), F), ((RR, N), F)] + [((RR + GR, N), B)] * 3,
        smem=1,
        name="join",
    )(place, keep_g, keep_r, got)
    arrived = [swap(x, "y", k + 1) for k, x in enumerate(outs)]
    (piece,) = call(sum_kernel, [((RR + GR, N), B)], name="sum")(own_g, own_r, *arrived)
    (line,) = call(line_kernel, [((4, RR + GR, N), B)], smem=1, name="line")(
        place, piece, *[swap(piece, "y", k) for k in (1, 2, 3)]
    )
    line, left_o, weight_o = lax.optimization_barrier((line, left_o, weight_o))
    other_core = swap(line, "c")
    (raw,) = call(rows_kernel, [((8 * RR, N), B)], smem=1, name="rows")(place, line, other_core)
    raw_o = swap(raw, "r")

    w16, ortho, right, squares = call(
        solve_kernel,
        [((384, N), B), ((N, N), B), ((8 * RR, N), F), ((1, N), F)],
        [pltpu.VMEM((N, N), F), pltpu.VMEM((N, N), F)],
        smem=1,
        name="solve",
    )(place, line, other_core, left, raw)
    w16_o = swap(w16, "r")
    sums = exchange(jnp.broadcast_to(squares[None], (32, 1, N)), ("x", "z", "r"))
    wide, tall = weight.shape, right.shape
    weight_new, moment_new, basis_new, rollout = call(
        last_kernel,
        [(wide, B), (wide, F), (tall, F), ((2, *wide), B)],
        [pltpu.VMEM((2, *wide), B), pltpu.VMEM(wide, F), pltpu.VMEM(tall, F), pltpu.VMEM((N, N), B), pltpu.SemaphoreType.DMA((5,))],
        smem=1,
        name="last",
        mib=24,
        out_spec=pl.BlockSpec(memory_space=pl.ANY),
    )(place, sums, momentum, gradient, ortho, right, left, w16, raw, weights[0], left_o, w16_o, raw_o, weight_o)
    return weight_new[None], moment_new[None], basis_new[None], rollout


def solution(mesh):
    finer = Mesh(mesh.devices.reshape(4, 2, 2, 8, 2), ("y", "c", "x", "z", "r"))
    split_specs = P("r", FSDP, TP)
    basis_spec = P("r", TP, None)
    return jax.shard_map(
        body,
        mesh=finer,
        in_specs=(split_specs, split_specs, split_specs, basis_spec),
        out_specs=(split_specs, split_specs, basis_spec, P(None, FSDP, TP)),
        check_vma=False,
    )
```

```python
import jax
import jax.numpy as jnp
from jax import lax
from jax.experimental import pallas as pl
from jax.experimental.pallas import tpu as pltpu
from jax.sharding import Mesh
from jax.sharding import PartitionSpec as P

COLS = 14336
TP = ("x", "z")
FSDP = ("y", "c")
F = jnp.float32
B = jnp.bfloat16
N = 512
NB = 128
GRP = 8
GR = 96
RR = 112
VMEM = pl.BlockSpec(memory_space=pltpu.VMEM)
SMEM = pl.BlockSpec(memory_space=pltpu.SMEM)


def call(kernel, outs, scratch=(), smem=0, name=None, mib=12, out_spec=VMEM):
    def run(*args):
        return pl.pallas_call(
            kernel,
            out_shape=[jax.ShapeDtypeStruct(s, d) for s, d in outs],
            in_specs=[SMEM] * smem + [VMEM] * (len(args) - smem),
            out_specs=[out_spec] * len(outs),
            scratch_shapes=list(scratch),
            compiler_params=pltpu.CompilerParams(vmem_limit_bytes=mib * 2**20),
            name=name,
        )(*args)

    return run


def dot(p, q, over):
    return lax.dot_general(p, q, (over, ((), ())), preferred_element_type=F)


NN, NT, TN = ((1,), (0,)), ((1,), (1,)), ((0,), (0,))


def halves(x):
    hi = x.astype(B)
    return hi, (x - hi.astype(F)).astype(B)


def dot3(a, b, over):
    ah, al = halves(a)
    bh, bl = halves(b)
    return dot(ah, bh, over) + (dot(ah, bl, over) + dot(al, bh, over))


def total(v):
    while len(v) > 1:
        v = [v[i] + v[i + 1] if i + 1 < len(v) else v[i] for i in range(0, len(v), 2)]
    return v[0]


def factor(rows):
    n, w, b = len(rows), rows[0].shape[1], GRP
    sub = lax.broadcasted_iota(jnp.int32, (8, w), 0)
    lane = lax.broadcasted_iota(jnp.int32, (8, w), 1)
    full = lambda v: jnp.broadcast_to(v, (8, w))
    for p in range(n):
        j = 8 * p
        cols = [full(rows[p][:, j + m : j + m + 1]) for m in range(b)]
        d = [[full(cols[m][i : i + 1, :]) for m in range(i + 1)] for i in range(b)]
        group = (lane >= j) & (lane < j + b)
        own = jnp.where(group, jnp.where(lane == sub + j, 1.0, 0.0), rows[p])
        row = [full(own[m : m + 1, :]) for m in range(b)]
        v = [[None] * b for _ in range(b)]
        low = [[None] * b for _ in range(b)]
        for i in range(b):
            rt = lax.rsqrt(d[i][i])
            for m in range(i + 1, b):
                low[m][i] = d[m][i] * rt
            for m in range(i + 1, b):
                for t in range(i + 1, m + 1):
                    d[m][t] = d[m][t] - low[m][i] * low[t][i]
            v[i][i] = rt
            for t in range(i):
                v[i][t] = -(rt * total([low[i][k] * v[k][t] for k in range(t, i)]))
        r = [total([v[i][m] * row[m] for m in range(i + 1)]) for i in range(b)]
        z = [total([v[i][m] * r[i] for i in range(m, b)]) for m in range(b)]
        for q in range(p + 1, min(p + 2, n)):
            c = [full(rows[q][:, j + m : j + m + 1]) for m in range(b)]
            rows[q] = jnp.where(group, 0.0, rows[q]) - total([c[m] * z[m] for m in range(b)])
        if p + 2 < n:
            far = jnp.concatenate(rows[p + 2 :], axis=0)
            terms = z[0]
            for m in range(1, b):
                terms = jnp.where(sub == m, z[m], terms)
            update = dot3(jnp.where(group[:1], far, 0.0), jnp.concatenate([terms] * (w // 8), axis=0), NN)
            far = jnp.where(group[:1], 0.0, far) - update
            for q in range(p + 2, n):
                rows[q] = far[8 * (q - p - 2) : 8 * (q - p - 1), :]
        y = r[0]
        for i in range(1, b):
            y = jnp.where(sub == i, r[i], y)
        rows[p] = jnp.where(lane < j + b, y, 0.0)
    return rows


def inverse_factor(a_ref, w_ref):
    for lo in range(0, N, NB):
        hi = lo + NB
        rows = [a_ref[lo + 8 * p : lo + 8 * p + 8, lo:hi] for p in range(NB // 8)]
        wkk = jnp.concatenate(factor(rows), axis=0)
        w_ref[lo:hi, lo:hi] = wkk
        if hi < N:
            w_ref[lo:hi, hi:] = jnp.zeros((NB, N - hi), F)
        if lo > 0:
            w_ref[lo:hi, :lo] = dot3(wkk, w_ref[lo:hi, :lo], NN)
        if hi < N:
            r = dot3(wkk, a_ref[lo:hi, hi:], NN)
            for s in range(hi, N, NB):
                a_ref[s : s + NB, s:] = a_ref[s : s + NB, s:] - dot3(r[:, s - hi : s - hi + NB], r[:, s - hi :], TN)
            upd = dot3(r, w_ref[lo:hi, :hi], TN)
            if lo > 0:
                w_ref[hi:, :lo] = w_ref[hi:, :lo] - upd[:, :lo]
            w_ref[hi:, lo:hi] = -upd[:, lo:]


def front_kernel(momentum, gradient, basis, part, blend, basis16):
    @pl.when(pl.program_id(0) == 0)
    def _():
        basis16[...] = basis[...].astype(B)

    x = (momentum[...] + gradient[...].astype(F)).astype(B)
    blend[...] = x
    part[...] = dot(x, basis16[...], NN).astype(B)


def front(momentum, gradient, basis):
    rows, cols = momentum.shape
    step = rows // 4
    return pl.pallas_call(
        front_kernel,
        grid=(4,),
        out_shape=[jax.ShapeDtypeStruct((rows, N), B), jax.ShapeDtypeStruct((rows, cols), B)],
        in_specs=[
            pl.BlockSpec((step, cols), lambda i: (i, 0)),
            pl.BlockSpec((step, cols), lambda i: (i, 0)),
            pl.BlockSpec((cols, N), lambda i: (0, 0)),
        ],
        out_specs=[pl.BlockSpec((step, N), lambda i: (i, 0)), pl.BlockSpec((step, cols), lambda i: (i, 0))],
        scratch_shapes=[pltpu.VMEM((cols, N), B)],
        compiler_params=pltpu.CompilerParams(vmem_limit_bytes=16 * 2**20),
        name="front",
    )(momentum, gradient, basis)


def spread_kernel(pieces, out):
    share = pieces[0].astype(F)
    for k in range(1, pieces.shape[0]):
        share = share + pieces[k].astype(F)
    share = share.astype(B)
    for k in range(out.shape[0]):
        out[k] = share


def pieces_kernel(place, left_ref, blend_ref, keep_g, keep_r, send, right_scr, part):
    right_scr[...] = dot(blend_ref[...], left_ref[...], TN)
    for mine in (True, False):
        c = place[1] if mine else 1 - place[1]
        wide = left_ref[:, pl.ds(pl.multiple_of(c * 256, 256), 256)]
        narrow = left_ref[:, pl.ds(pl.multiple_of(c * 128, 128), 128)]
        part[:256, :] = dot(wide, wide, TN)
        part[256:, :] = dot(narrow, left_ref[:, 256:], TN)
        for y in range(4):
            g = part[y * GR : (y + 1) * GR, :]
            r = right_scr[pl.ds(pl.multiple_of((2 * y + c) * RR, 16), RR), :]
            if mine:
                keep_g[y] = g
                keep_r[y] = r
            else:
                packed(send.at[y], g, r)


def packed(out, g, r):
    gh, gl = halves(g)
    out[:RR, :] = r.astype(B)
    out[RR:, :256] = gh
    out[RR:, 256:] = gl


def gram_of(ref):
    return ref[RR:, :256].astype(F) + ref[RR:, 256:].astype(F)


def join_kernel(place, keep_g, keep_r, got, own_g, own_r, one, two, three):
    for k, out in enumerate((None, one, two, three)):
        y = place[0] ^ k
        r = keep_r[y] + got[y, :RR, :].astype(F)
        g = keep_g[y] + gram_of(got.at[y])
        if out is None:
            own_g[...] = g
            own_r[...] = r
        else:
            packed(out, g, r)


def sum_kernel(own_g, own_r, one, two, three, out):
    g, r = own_g[...], own_r[...]
    for got in (one, two, three):
        r = r + got[:RR, :].astype(F)
        g = g + gram_of(got)
    packed(out, g, r)


def line_kernel(place, own, one, two, three, out):
    for k, got in enumerate((own, one, two, three)):
        out[place[0] ^ k] = got[...]


def rows_kernel(place, own, got, right):
    for y in range(4):
        for c, part in ((place[1], own), (1 - place[1], got)):
            right[pl.ds(pl.multiple_of((2 * y + c) * RR, 16), RR), :] = part[y, :RR, :]


def solve_kernel(place, own, got, left, right_in, w16, ortho, right, squares, a, w):
    for y in range(4):
        first = y * GR
        square = max(0, min(GR, 256 - first))
        for c, part in ((place[1], own), (1 - place[1], got)):
            g = gram_of(part.at[y])
            if square:
                rows = pl.ds(pl.multiple_of(c * 256 + first, 32), square)
                a[rows, pl.ds(pl.multiple_of(c * 256, 256), 256)] = g[:square, :]
            if square < GR:
                rows = pl.ds(pl.multiple_of(c * 128 + first + square - 256, 32), GR - square)
                a[rows, 256:] = g[square:, :]
    inverse_factor(a, w)
    wh, wl = halves(w[...])
    w16[:256, :] = wh[256:, :]
    w16[256:, :256] = wh[:128, :256]
    w16[256:, 256:] = wh[128:256, :256]
    ortho[...] = (dot(left[...], wh, NT) + dot(left[...], wl, NT)).astype(B)
    r = dot(right_in[...], wh, NT) + dot(right_in[...], wl, NT)
    right[...] = r
    squares[...] = jnp.sum(r * r, axis=0, keepdims=True)


def last_kernel(
    place, sums, momentum, gradient, ortho, right, left0, w0, right0, weight0, left1, w1, right1, weight1,
    out_weight, out_moment, out_basis, out_rollout, weight, moment, basis, w, sems,
):
    scales = []
    for side in range(2):
        squares = sums[side]
        for k in range(2 + side, 32, 2):
            squares = squares + sums[k]
        scales.append(lax.rsqrt(squares / COLS + 1e-06))
    first = place[2] == 0
    scale = [jnp.where(first, *scales), jnp.where(first, *scales[::-1])]
    basis[...] = right[...] * scale[0]
    copies = [pltpu.make_async_copy(basis, out_basis, sems.at[0])]
    copies[-1].start()
    blend = momentum[...] + gradient[...].astype(F)
    moment[...] = blend - 0.05 * dot(ortho[...], right[...].astype(B), NT)
    copies.append(pltpu.make_async_copy(moment, out_moment, sems.at[1]))
    copies[-1].start()
    for half, refs in enumerate(((left0, w0, right0, weight0), (left1, w1, right1, weight1))):
        left, packed_w, raw, old = refs
        w[256:, :] = packed_w[:256, :]
        w[:128, :256] = packed_w[256:, :256]
        w[128:256, :256] = packed_w[256:, 256:]
        w[:256, 256:] = jnp.zeros((256, 256), B)
        o = (dot(left[...], w[...], NT) * scale[half]).astype(B)
        r = dot(raw[...], w[...], NT).astype(B)
        weight[half] = (old[...].astype(F) - 0.3 * dot(o, r, NT)).astype(B)
        side = place[2] if half == 0 else 1 - place[2]
        copies.append(pltpu.make_async_copy(weight.at[half], out_rollout.at[side], sems.at[2 + half]))
        copies[-1].start()
        if half == 0:
            copies.append(pltpu.make_async_copy(weight.at[0], out_weight, sems.at[4]))
            copies[-1].start()
    for copy in copies:
        copy.wait()


def exchange(x, axis):
    return lax.all_to_all(x, axis, 0, 0, tiled=True)


def swap(x, axis, bit=1):
    return lax.ppermute(x, axis, [(i, i ^ bit) for i in range(lax.axis_size(axis))])


def body(weights, gradient, momentum, basis):
    place = jnp.stack([lax.axis_index(axis) for axis in ("y", "c", "r")]).astype(jnp.int32)
    place, basis = lax.optimization_barrier((place, basis))
    momentum, gradient = momentum[0], gradient[0]
    part, blend16 = front(momentum, gradient, basis[0])
    part = part.reshape(16, -1, N)
    (copies,) = call(spread_kernel, [(part.shape, B)], name="spread")(exchange(part, TP))
    left = exchange(copies, TP).reshape(-1, N)

    keep_g, keep_r, send = call(
        pieces_kernel,
        [((4, GR, 256), F), ((4, RR, N), F), ((4, RR + GR, N), B)],
        [pltpu.VMEM((8 * RR, N), F), pltpu.VMEM((384, 256), F)],
        smem=1,
        name="pieces",
    )(place, left, blend16)
    got = swap(send, "c")
    own_g, own_r, *outs = call(
        join_kernel,
        [((GR, 256), F), ((RR, N), F)] + [((RR + GR, N), B)] * 3,
        smem=1,
        name="join",
    )(place, keep_g, keep_r, got)
    early_left, weight, *outs = lax.optimization_barrier((left, weights[0], *outs))
    left_o, weight_o = swap(early_left, "r"), swap(weight, "r")
    arrived = [swap(x, "y", k + 1) for k, x in enumerate(outs)]
    (piece,) = call(sum_kernel, [((RR + GR, N), B)], name="sum")(own_g, own_r, *arrived)
    (line,) = call(line_kernel, [((4, RR + GR, N), B)], smem=1, name="line")(
        place, piece, *[swap(piece, "y", k) for k in (1, 2, 3)]
    )
    other_core = swap(line, "c")
    (raw,) = call(rows_kernel, [((8 * RR, N), B)], smem=1, name="rows")(place, line, other_core)
    raw_o = swap(raw, "r")
    left, left_o, weight_o = lax.optimization_barrier((left, left_o, weight_o))

    w16, ortho, right, squares = call(
        solve_kernel,
        [((384, N), B), ((N, N), B), ((8 * RR, N), F), ((1, N), F)],
        [pltpu.VMEM((N, N), F), pltpu.VMEM((N, N), F)],
        smem=1,
        name="solve",
    )(place, line, other_core, left, raw)
    w16_o = swap(w16, "r")
    sums = exchange(jnp.broadcast_to(squares[None], (32, 1, N)), ("x", "z", "r"))
    wide, tall = weight.shape, right.shape
    weight_new, moment_new, basis_new, rollout = call(
        last_kernel,
        [(wide, B), (wide, F), (tall, F), ((2, *wide), B)],
        [pltpu.VMEM((2, *wide), B), pltpu.VMEM(wide, F), pltpu.VMEM(tall, F), pltpu.VMEM((N, N), B), pltpu.SemaphoreType.DMA((5,))],
        smem=1,
        name="last",
        mib=24,
        out_spec=pl.BlockSpec(memory_space=pl.ANY),
    )(place, sums, momentum, gradient, ortho, right, left, w16, raw, weights[0], left_o, w16_o, raw_o, weight_o)
    return weight_new[None], moment_new[None], basis_new[None], rollout


def solution(mesh):
    finer = Mesh(mesh.devices.reshape(4, 2, 2, 8, 2), ("y", "c", "x", "z", "r"))
    split_specs = P("r", FSDP, TP)
    basis_spec = P("r", TP, None)
    return jax.shard_map(
        body,
        mesh=finer,
        in_specs=(split_specs, split_specs, split_specs, basis_spec),
        out_specs=(split_specs, split_specs, basis_spec, P(None, FSDP, TP)),
        check_vma=False,
    )
```

```python
import jax
import jax.numpy as jnp
from jax import lax
from jax.experimental import pallas as pl
from jax.experimental.pallas import tpu as pltpu
from jax.sharding import Mesh
from jax.sharding import PartitionSpec as P

COLS = 14336
TP = ("x", "z")
FSDP = ("y", "c")
F = jnp.float32
B = jnp.bfloat16
N = 512
NB = 128
GRP = 8
GR = 96
RR = 112
EARLY = 384
VMEM = pl.BlockSpec(memory_space=pltpu.VMEM)
SMEM = pl.BlockSpec(memory_space=pltpu.SMEM)


def call(kernel, outs, scratch=(), smem=0, name=None, mib=12, out_spec=VMEM):
    def run(*args):
        return pl.pallas_call(
            kernel,
            out_shape=[jax.ShapeDtypeStruct(s, d) for s, d in outs],
            in_specs=[SMEM] * smem + [VMEM] * (len(args) - smem),
            out_specs=[out_spec] * len(outs),
            scratch_shapes=list(scratch),
            compiler_params=pltpu.CompilerParams(vmem_limit_bytes=mib * 2**20),
            name=name,
        )(*args)

    return run


def dot(p, q, over):
    return lax.dot_general(p, q, (over, ((), ())), preferred_element_type=F)


NN, NT, TN = ((1,), (0,)), ((1,), (1,)), ((0,), (0,))


def halves(x):
    hi = x.astype(B)
    return hi, (x - hi.astype(F)).astype(B)


def dot3(a, b, over):
    ah, al = halves(a)
    bh, bl = halves(b)
    return dot(ah, bh, over) + (dot(ah, bl, over) + dot(al, bh, over))


def total(v):
    while len(v) > 1:
        v = [v[i] + v[i + 1] if i + 1 < len(v) else v[i] for i in range(0, len(v), 2)]
    return v[0]


def factor(rows):
    n, w, b = len(rows), rows[0].shape[1], GRP
    sub = lax.broadcasted_iota(jnp.int32, (8, w), 0)
    lane = lax.broadcasted_iota(jnp.int32, (8, w), 1)
    full = lambda v: jnp.broadcast_to(v, (8, w))
    for p in range(n):
        j = 8 * p
        cols = [full(rows[p][:, j + m : j + m + 1]) for m in range(b)]
        d = [[full(cols[m][i : i + 1, :]) for m in range(i + 1)] for i in range(b)]
        group = (lane >= j) & (lane < j + b)
        own = jnp.where(group, jnp.where(lane == sub + j, 1.0, 0.0), rows[p])
        row = [full(own[m : m + 1, :]) for m in range(b)]
        v = [[None] * b for _ in range(b)]
        low = [[None] * b for _ in range(b)]
        for i in range(b):
            rt = lax.rsqrt(d[i][i])
            for m in range(i + 1, b):
                low[m][i] = d[m][i] * rt
            for m in range(i + 1, b):
                for t in range(i + 1, m + 1):
                    d[m][t] = d[m][t] - low[m][i] * low[t][i]
            v[i][i] = rt
            for t in range(i):
                v[i][t] = -(rt * total([low[i][k] * v[k][t] for k in range(t, i)]))
        r = [total([v[i][m] * row[m] for m in range(i + 1)]) for i in range(b)]
        z = [total([v[i][m] * r[i] for i in range(m, b)]) for m in range(b)]
        for q in range(p + 1, min(p + 2, n)):
            c = [full(rows[q][:, j + m : j + m + 1]) for m in range(b)]
            rows[q] = jnp.where(group, 0.0, rows[q]) - total([c[m] * z[m] for m in range(b)])
        if p + 2 < n:
            far = jnp.concatenate(rows[p + 2 :], axis=0)
            terms = z[0]
            for m in range(1, b):
                terms = jnp.where(sub == m, z[m], terms)
            update = dot3(jnp.where(group[:1], far, 0.0), jnp.concatenate([terms] * (w // 8), axis=0), NN)
            far = jnp.where(group[:1], 0.0, far) - update
            for q in range(p + 2, n):
                rows[q] = far[8 * (q - p - 2) : 8 * (q - p - 1), :]
        y = r[0]
        for i in range(1, b):
            y = jnp.where(sub == i, r[i], y)
        rows[p] = jnp.where(lane < j + b, y, 0.0)
    return rows


def inverse_factor(a_ref, w_ref):
    for lo in range(0, N, NB):
        hi = lo + NB
        rows = [a_ref[lo + 8 * p : lo + 8 * p + 8, lo:hi] for p in range(NB // 8)]
        wkk = jnp.concatenate(factor(rows), axis=0)
        w_ref[lo:hi, lo:hi] = wkk
        if hi < N:
            w_ref[lo:hi, hi:] = jnp.zeros((NB, N - hi), F)
        if lo > 0:
            w_ref[lo:hi, :lo] = dot3(wkk, w_ref[lo:hi, :lo], NN)
        if hi < N:
            r = dot3(wkk, a_ref[lo:hi, hi:], NN)
            for s in range(hi, N, NB):
                a_ref[s : s + NB, s:] = a_ref[s : s + NB, s:] - dot3(r[:, s - hi : s - hi + NB], r[:, s - hi :], TN)
            upd = dot3(r, w_ref[lo:hi, :hi], TN)
            if lo > 0:
                w_ref[hi:, :lo] = w_ref[hi:, :lo] - upd[:, :lo]
            w_ref[hi:, lo:hi] = -upd[:, lo:]


def front_kernel(momentum, gradient, basis, part, blend, m_ref, g_ref, b_ref, sems):
    steps = 4
    step = m_ref.shape[0] // steps
    copies = [pltpu.make_async_copy(basis, b_ref, sems.at[2 * steps])]
    for k in range(steps):
        rows = pl.ds(k * step, step)
        copies.append(pltpu.make_async_copy(momentum.at[rows], m_ref.at[rows], sems.at[2 * k]))
        copies.append(pltpu.make_async_copy(gradient.at[rows], g_ref.at[rows], sems.at[2 * k + 1]))
    for copy in copies:
        copy.start()
    copies[0].wait()
    basis16 = b_ref[...].astype(B)
    for k in range(steps):
        copies[2 * k + 1].wait()
        copies[2 * k + 2].wait()
        rows = pl.ds(k * step, step)
        x = (m_ref[rows] + g_ref[rows].astype(F)).astype(B)
        blend[rows] = x
        part[rows] = dot(x, basis16, NN).astype(B)


def front(momentum, gradient, basis):
    rows, cols = momentum.shape
    return pl.pallas_call(
        front_kernel,
        out_shape=[jax.ShapeDtypeStruct((rows, N), B), jax.ShapeDtypeStruct((rows, cols), B)],
        in_specs=[pl.BlockSpec(memory_space=pltpu.HBM)] * 3,
        out_specs=[VMEM] * 2,
        scratch_shapes=[
            pltpu.VMEM((rows, cols), F),
            pltpu.VMEM((rows, cols), B),
            pltpu.VMEM((cols, N), F),
            pltpu.SemaphoreType.DMA((9,)),
        ],
        compiler_params=pltpu.CompilerParams(vmem_limit_bytes=60 * 2**20),
        name="front",
    )(momentum, gradient, basis)


def spread_kernel(pieces, out):
    share = pieces[0].astype(F)
    for k in range(1, pieces.shape[0]):
        share = share + pieces[k].astype(F)
    share = share.astype(B)
    for k in range(out.shape[0]):
        out[k] = share


def pieces_kernel(place, left_ref, blend_ref, keep_g, keep_r, send, right_scr, part):
    right_scr[...] = dot(blend_ref[...], left_ref[...], TN)
    for mine in (True, False):
        c = place[1] if mine else 1 - place[1]
        wide = left_ref[:, pl.ds(pl.multiple_of(c * 256, 256), 256)]
        narrow = left_ref[:, pl.ds(pl.multiple_of(c * 128, 128), 128)]
        part[:256, :] = dot(wide, wide, TN)
        part[256:, :] = dot(narrow, left_ref[:, 256:], TN)
        for y in range(4):
            g = part[y * GR : (y + 1) * GR, :]
            r = right_scr[pl.ds(pl.multiple_of((2 * y + c) * RR, 16), RR), :]
            if mine:
                keep_g[y] = g
                keep_r[y] = r
            else:
                packed(send.at[y], g, r)


def packed(out, g, r):
    gh, gl = halves(g)
    out[:RR, :] = r.astype(B)
    out[RR:, :256] = gh
    out[RR:, 256:] = gl


def gram_of(ref):
    return ref[RR:, :256].astype(F) + ref[RR:, 256:].astype(F)


def join_kernel(place, keep_g, keep_r, got, own_g, own_r, one, two, three):
    for k, out in enumerate((None, one, two, three)):
        y = place[0] ^ k
        r = keep_r[y] + got[y, :RR, :].astype(F)
        g = keep_g[y] + gram_of(got.at[y])
        if out is None:
            own_g[...] = g
            own_r[...] = r
        else:
            packed(out, g, r)


def sum_kernel(own_g, own_r, one, two, three, out):
    g, r = own_g[...], own_r[...]
    for got in (one, two, three):
        r = r + got[:RR, :].astype(F)
        g = g + gram_of(got)
    packed(out, g, r)


def line_kernel(place, own, one, two, three, out):
    for k, got in enumerate((own, one, two, three)):
        out[place[0] ^ k] = got[...]


def rows_kernel(place, own, got, weight, right):
    late = weight.shape[0] - EARLY
    wide = weight.shape[1] - N
    right[8 * RR : 8 * RR + late, :] = weight[EARLY:, :N]
    right[8 * RR + late :, :wide] = weight[EARLY:, N:]
    right[8 * RR + late :, wide:] = jnp.zeros((late, N - wide), B)
    for y in range(4):
        for c, part in ((place[1], own), (1 - place[1], got)):
            right[pl.ds(pl.multiple_of((2 * y + c) * RR, 16), RR), :] = part[y, :RR, :]


def solve_kernel(place, own, got, left, right_in, w16, ortho, right, squares, a, w):
    for y in range(4):
        first = y * GR
        square = max(0, min(GR, 256 - first))
        for c, part in ((place[1], own), (1 - place[1], got)):
            g = gram_of(part.at[y])
            if square:
                rows = pl.ds(pl.multiple_of(c * 256 + first, 32), square)
                a[rows, pl.ds(pl.multiple_of(c * 256, 256), 256)] = g[:square, :]
            if square < GR:
                rows = pl.ds(pl.multiple_of(c * 128 + first + square - 256, 32), GR - square)
                a[rows, 256:] = g[square:, :]
    inverse_factor(a, w)
    wh, wl = halves(w[...])
    w16[:256, :] = wh[256:, :]
    w16[256:, :256] = wh[:128, :256]
    w16[256:, 256:] = wh[128:256, :256]
    ortho[...] = (dot(left[...], wh, NT) + dot(left[...], wl, NT)).astype(B)
    raw = right_in[: 8 * RR, :]
    r = dot(raw, wh, NT) + dot(raw, wl, NT)
    right[...] = r
    squares[...] = jnp.sum(r * r, axis=0, keepdims=True)


def last_kernel(
    place, sums, momentum, gradient, ortho, right, left0, w0, right0, weight0, left1, w1, right1, weight1,
    out_weight, out_moment, out_basis, out_rollout, weight, moment, basis, w, sems,
):
    scales = []
    for side in range(2):
        squares = sums[side]
        for k in range(2 + side, 32, 2):
            squares = squares + sums[k]
        scales.append(lax.rsqrt(squares / COLS + 1e-06))
    first = place[2] == 0
    scale = [jnp.where(first, *scales), jnp.where(first, *scales[::-1])]
    basis[...] = right[...] * scale[0]
    copies = [pltpu.make_async_copy(basis, out_basis, sems.at[0])]
    copies[-1].start()
    blend = momentum[...] + gradient[...].astype(F)
    moment[...] = blend - 0.05 * dot(ortho[...], right[...].astype(B), NT)
    copies.append(pltpu.make_async_copy(moment, out_moment, sems.at[1]))
    copies[-1].start()
    for half, refs in enumerate(((left0, w0, right0, weight0), (left1, w1, right1, weight1))):
        left, packed_w, raw, old = refs
        w[256:, :] = packed_w[:256, :]
        w[:128, :256] = packed_w[256:, :256]
        w[128:256, :256] = packed_w[256:, 256:]
        w[:256, 256:] = jnp.zeros((256, 256), B)
        o = (dot(left[...], w[...], NT) * scale[half]).astype(B)
        r = dot(raw[: 8 * RR, :], w[...], NT).astype(B)
        update = 0.3 * dot(o, r, NT)
        if half == 0:
            weight[half] = (old[...].astype(F) - update).astype(B)
        else:
            late, wide = update.shape[0] - EARLY, update.shape[1] - N
            weight[half, :EARLY] = (old[...].astype(F) - update[:EARLY]).astype(B)
            low, high = raw[8 * RR : 8 * RR + late, :], raw[8 * RR + late :, :wide]
            weight[half, EARLY:, :N] = (low.astype(F) - update[EARLY:, :N]).astype(B)
            weight[half, EARLY:, N:] = (high.astype(F) - update[EARLY:, N:]).astype(B)
        side = place[2] if half == 0 else 1 - place[2]
        copies.append(pltpu.make_async_copy(weight.at[half], out_rollout.at[side], sems.at[2 + half]))
        copies[-1].start()
        if half == 0:
            copies.append(pltpu.make_async_copy(weight.at[0], out_weight, sems.at[4]))
            copies[-1].start()
    for copy in copies:
        copy.wait()


def exchange(x, axis):
    return lax.all_to_all(x, axis, 0, 0, tiled=True)


def swap(x, axis, bit=1):
    return lax.ppermute(x, axis, [(i, i ^ bit) for i in range(lax.axis_size(axis))])


def body(weights, gradient, momentum, basis):
    place = jnp.stack([lax.axis_index(axis) for axis in ("y", "c", "r")]).astype(jnp.int32)
    place, basis = lax.optimization_barrier((place, basis))
    momentum, gradient = momentum[0], gradient[0]
    part, blend16 = front(momentum, gradient, basis[0])
    part = part.reshape(16, -1, N)
    (copies,) = call(spread_kernel, [(part.shape, B)], name="spread")(exchange(part, TP))
    left = exchange(copies, TP).reshape(-1, N)

    keep_g, keep_r, send = call(
        pieces_kernel,
        [((4, GR, 256), F), ((4, RR, N), F), ((4, RR + GR, N), B)],
        [pltpu.VMEM((8 * RR, N), F), pltpu.VMEM((384, 256), F)],
        smem=1,
        name="pieces",
    )(place, left, blend16)
    got = swap(send, "c")
    left_o = swap(left, "r")
    weight, _ = lax.optimization_barrier((weights[0, :EARLY], left))
    weight_o = swap(weight, "r")
    own_g, own_r, *outs = call(
        join_kernel,
        [((GR, 256), F), ((RR, N), F)] + [((RR + GR, N), B)] * 3,
        smem=1,
        name="join",
    )(place, keep_g, keep_r, got)
    arrived = [swap(x, "y", k + 1) for k, x in enumerate(outs)]
    (piece,) = call(sum_kernel, [((RR + GR, N), B)], name="sum")(own_g, own_r, *arrived)
    (line,) = call(line_kernel, [((4, RR + GR, N), B)], smem=1, name="line")(
        place, piece, *[swap(piece, "y", k) for k in (1, 2, 3)]
    )
    line, left_o, weight_o = lax.optimization_barrier((line, left_o, weight_o))
    other_core = swap(line, "c")
    late = 2 * (weights.shape[1] - EARLY)
    (raw,) = call(rows_kernel, [((8 * RR + late, N), B)], smem=1, name="rows")(place, line, other_core, weights[0])
    raw_o = swap(raw, "r")

    w16, ortho, right, squares = call(
        solve_kernel,
        [((384, N), B), ((N, N), B), ((8 * RR, N), F), ((1, N), F)],
        [pltpu.VMEM((N, N), F), pltpu.VMEM((N, N), F)],
        smem=1,
        name="solve",
    )(place, line, other_core, left, raw)
    w16_o = swap(w16, "r")
    sums = exchange(jnp.broadcast_to(squares[None], (32, 1, N)), ("x", "z", "r"))
    wide, tall = momentum.shape, right.shape
    weight_new, moment_new, basis_new, rollout = call(
        last_kernel,
        [(wide, B), (wide, F), (tall, F), ((2, *wide), B)],
        [pltpu.VMEM((2, *wide), B), pltpu.VMEM(wide, F), pltpu.VMEM(tall, F), pltpu.VMEM((N, N), B), pltpu.SemaphoreType.DMA((5,))],
        smem=1,
        name="last",
        mib=24,
        out_spec=pl.BlockSpec(memory_space=pl.ANY),
    )(place, sums, momentum, gradient, ortho, right, left, w16, raw, weights[0], left_o, w16_o, raw_o, weight_o)
    return weight_new[None], moment_new[None], basis_new[None], rollout


def solution(mesh):
    finer = Mesh(mesh.devices.reshape(4, 2, 2, 8, 2), ("y", "c", "x", "z", "r"))
    split_specs = P("r", FSDP, TP)
    basis_spec = P("r", TP, None)
    return jax.shard_map(
        body,
        mesh=finer,
        in_specs=(split_specs, split_specs, split_specs, basis_spec),
        out_specs=(split_specs, split_specs, basis_spec, P(None, FSDP, TP)),
        check_vma=False,
    )
```

```python
import jax
import jax.numpy as jnp
from jax import lax
from jax.experimental import pallas as pl
from jax.experimental.pallas import tpu as pltpu
from jax.sharding import Mesh
from jax.sharding import PartitionSpec as P

COLS = 14336
TP = ("x", "z")
FSDP = ("y", "c")
F = jnp.float32
B = jnp.bfloat16
N = 512
NB = 128
GRP = 8
GR = 96
RR = 112
EARLY = 384
VMEM = pl.BlockSpec(memory_space=pltpu.VMEM)
SMEM = pl.BlockSpec(memory_space=pltpu.SMEM)


def call(kernel, outs, scratch=(), smem=0, name=None, mib=12, out_spec=VMEM):
    def run(*args):
        return pl.pallas_call(
            kernel,
            out_shape=[jax.ShapeDtypeStruct(s, d) for s, d in outs],
            in_specs=[SMEM] * smem + [VMEM] * (len(args) - smem),
            out_specs=[out_spec] * len(outs),
            scratch_shapes=list(scratch),
            compiler_params=pltpu.CompilerParams(vmem_limit_bytes=mib * 2**20),
            name=name,
        )(*args)

    return run


def dot(p, q, over):
    return lax.dot_general(p, q, (over, ((), ())), preferred_element_type=F)


NN, NT, TN = ((1,), (0,)), ((1,), (1,)), ((0,), (0,))


def halves(x):
    hi = x.astype(B)
    return hi, (x - hi.astype(F)).astype(B)


def dot3(a, b, over):
    ah, al = halves(a)
    bh, bl = halves(b)
    return dot(ah, bh, over) + (dot(ah, bl, over) + dot(al, bh, over))


def total(v):
    while len(v) > 1:
        v = [v[i] + v[i + 1] if i + 1 < len(v) else v[i] for i in range(0, len(v), 2)]
    return v[0]


def factor(rows):
    n, w, b = len(rows), rows[0].shape[1], GRP
    sub = lax.broadcasted_iota(jnp.int32, (8, w), 0)
    lane = lax.broadcasted_iota(jnp.int32, (8, w), 1)
    full = lambda v: jnp.broadcast_to(v, (8, w))
    for p in range(n):
        j = 8 * p
        cols = [full(rows[p][:, j + m : j + m + 1]) for m in range(b)]
        d = [[full(cols[m][i : i + 1, :]) for m in range(i + 1)] for i in range(b)]
        group = (lane >= j) & (lane < j + b)
        own = jnp.where(group, jnp.where(lane == sub + j, 1.0, 0.0), rows[p])
        row = [full(own[m : m + 1, :]) for m in range(b)]
        v = [[None] * b for _ in range(b)]
        low = [[None] * b for _ in range(b)]
        for i in range(b):
            rt = lax.rsqrt(d[i][i])
            for m in range(i + 1, b):
                low[m][i] = d[m][i] * rt
            for m in range(i + 1, b):
                for t in range(i + 1, m + 1):
                    d[m][t] = d[m][t] - low[m][i] * low[t][i]
            v[i][i] = rt
            for t in range(i):
                v[i][t] = -(rt * total([low[i][k] * v[k][t] for k in range(t, i)]))
        r = [total([v[i][m] * row[m] for m in range(i + 1)]) for i in range(b)]
        z = [total([v[i][m] * r[i] for i in range(m, b)]) for m in range(b)]
        for q in range(p + 1, min(p + 2, n)):
            c = [full(rows[q][:, j + m : j + m + 1]) for m in range(b)]
            rows[q] = jnp.where(group, 0.0, rows[q]) - total([c[m] * z[m] for m in range(b)])
        if p + 2 < n:
            far = jnp.concatenate(rows[p + 2 :], axis=0)
            terms = z[0]
            for m in range(1, b):
                terms = jnp.where(sub == m, z[m], terms)
            update = dot3(jnp.where(group[:1], far, 0.0), jnp.concatenate([terms] * (w // 8), axis=0), NN)
            far = jnp.where(group[:1], 0.0, far) - update
            for q in range(p + 2, n):
                rows[q] = far[8 * (q - p - 2) : 8 * (q - p - 1), :]
        y = r[0]
        for i in range(1, b):
            y = jnp.where(sub == i, r[i], y)
        rows[p] = jnp.where(lane < j + b, y, 0.0)
    return rows


def inverse_factor(a_ref, w_ref):
    for lo in range(0, N, NB):
        hi = lo + NB
        rows = [a_ref[lo + 8 * p : lo + 8 * p + 8, lo:hi] for p in range(NB // 8)]
        wkk = jnp.concatenate(factor(rows), axis=0)
        w_ref[lo:hi, lo:hi] = wkk
        if hi < N:
            w_ref[lo:hi, hi:] = jnp.zeros((NB, N - hi), F)
        if lo > 0:
            w_ref[lo:hi, :lo] = dot3(wkk, w_ref[lo:hi, :lo], NN)
        if hi < N:
            r = dot3(wkk, a_ref[lo:hi, hi:], NN)
            for s in range(hi, N, NB):
                a_ref[s : s + NB, s:] = a_ref[s : s + NB, s:] - dot3(r[:, s - hi : s - hi + NB], r[:, s - hi :], TN)
            upd = dot3(r, w_ref[lo:hi, :hi], TN)
            if lo > 0:
                w_ref[hi:, :lo] = w_ref[hi:, :lo] - upd[:, :lo]
            w_ref[hi:, lo:hi] = -upd[:, lo:]


def front_kernel(momentum, gradient, basis, part, blend, m_ref, g_ref, b_ref, sems):
    steps = 4
    step = m_ref.shape[0] // steps
    copies = [pltpu.make_async_copy(basis, b_ref, sems.at[2 * steps])]
    for k in range(steps):
        rows = pl.ds(k * step, step)
        copies.append(pltpu.make_async_copy(momentum.at[rows], m_ref.at[rows], sems.at[2 * k]))
        copies.append(pltpu.make_async_copy(gradient.at[rows], g_ref.at[rows], sems.at[2 * k + 1]))
    for copy in copies:
        copy.start()
    copies[0].wait()
    basis16 = b_ref[...].astype(B)
    for k in range(steps):
        copies[2 * k + 1].wait()
        copies[2 * k + 2].wait()
        rows = pl.ds(k * step, step)
        x = (m_ref[rows] + g_ref[rows].astype(F)).astype(B)
        blend[rows] = x
        part[rows] = dot(x, basis16, NN).astype(B)


def front(momentum, gradient, basis):
    rows, cols = momentum.shape
    return pl.pallas_call(
        front_kernel,
        out_shape=[jax.ShapeDtypeStruct((rows, N), B), jax.ShapeDtypeStruct((rows, cols), B)],
        in_specs=[pl.BlockSpec(memory_space=pltpu.HBM)] * 3,
        out_specs=[VMEM] * 2,
        scratch_shapes=[
            pltpu.VMEM((rows, cols), F),
            pltpu.VMEM((rows, cols), B),
            pltpu.VMEM((cols, N), F),
            pltpu.SemaphoreType.DMA((9,)),
        ],
        compiler_params=pltpu.CompilerParams(vmem_limit_bytes=60 * 2**20),
        name="front",
    )(momentum, gradient, basis)


def spread_kernel(pieces, out):
    share = pieces[0].astype(F)
    for k in range(1, pieces.shape[0]):
        share = share + pieces[k].astype(F)
    share = share.astype(B)
    for k in range(out.shape[0]):
        out[k] = share


def pieces_kernel(place, left_ref, blend_ref, keep_g, keep_r, send, right_scr, part):
    right_scr[...] = dot(blend_ref[...], left_ref[...], TN)
    for mine in (True, False):
        c = place[1] if mine else 1 - place[1]
        wide = left_ref[:, pl.ds(pl.multiple_of(c * 256, 256), 256)]
        narrow = left_ref[:, pl.ds(pl.multiple_of(c * 128, 128), 128)]
        part[:256, :] = dot(wide, wide, TN)
        part[256:, :] = dot(narrow, left_ref[:, 256:], TN)
        for y in range(4):
            g = part[y * GR : (y + 1) * GR, :]
            r = right_scr[pl.ds(pl.multiple_of((2 * y + c) * RR, 16), RR), :]
            if mine:
                keep_g[y] = g
                keep_r[y] = r
            else:
                packed(send.at[y], g, r)


def packed(out, g, r):
    gh, gl = halves(g)
    out[:RR, :] = r.astype(B)
    out[RR:, :256] = gh
    out[RR:, 256:] = gl


def gram_of(ref):
    return ref[RR:, :256].astype(F) + ref[RR:, 256:].astype(F)


def join_kernel(place, keep_g, keep_r, got, own_g, own_r, one, two, three):
    for k, out in enumerate((None, one, two, three)):
        y = place[0] ^ k
        r = keep_r[y] + got[y, :RR, :].astype(F)
        g = keep_g[y] + gram_of(got.at[y])
        if out is None:
            own_g[...] = g
            own_r[...] = r
        else:
            packed(out, g, r)


def sum_kernel(own_g, own_r, one, two, three, out):
    g, r = own_g[...], own_r[...]
    for got in (one, two, three):
        r = r + got[:RR, :].astype(F)
        g = g + gram_of(got)
    packed(out, g, r)


def line_kernel(place, own, one, two, three, weight, out, half):
    late, wide = weight.shape[0] - EARLY, weight.shape[1] - N
    for k, got in enumerate((own, one, two, three)):
        y = place[0] ^ k
        out[y] = got[...]
        half[pl.ds(pl.multiple_of(y * RR, 16), RR), :] = got[:RR, :]
    half[4 * RR : 4 * RR + late, :] = weight[EARLY:, :N]
    half[4 * RR + late :, :wide] = weight[EARLY:, N:]
    half[4 * RR + late :, wide:] = jnp.zeros((late, N - wide), B)


def rows_kernel(place, own, got, right):
    for y in range(4):
        for c, part in ((place[1], own), (1 - place[1], got)):
            right[pl.ds(pl.multiple_of((2 * y + c) * RR, 16), RR), :] = part[y, :RR, :]


def solve_kernel(place, own, got, left, right_in, w16, ortho, right, squares, a, w):
    for y in range(4):
        first = y * GR
        square = max(0, min(GR, 256 - first))
        for c, part in ((place[1], own), (1 - place[1], got)):
            g = gram_of(part.at[y])
            if square:
                rows = pl.ds(pl.multiple_of(c * 256 + first, 32), square)
                a[rows, pl.ds(pl.multiple_of(c * 256, 256), 256)] = g[:square, :]
            if square < GR:
                rows = pl.ds(pl.multiple_of(c * 128 + first + square - 256, 32), GR - square)
                a[rows, 256:] = g[square:, :]
    inverse_factor(a, w)
    wh, wl = halves(w[...])
    w16[:256, :] = wh[256:, :]
    w16[256:, :256] = wh[:128, :256]
    w16[256:, 256:] = wh[128:256, :256]
    ortho[...] = (dot(left[...], wh, NT) + dot(left[...], wl, NT)).astype(B)
    r = dot(right_in[...], wh, NT) + dot(right_in[...], wl, NT)
    right[...] = r
    squares[...] = jnp.sum(r * r, axis=0, keepdims=True)


def last_kernel(
    place, sums, momentum, gradient, ortho, right, left0, w0, raw0, weight0, left1, w1, half1, half2, weight1,
    out_weight, out_moment, out_basis, out_rollout, weight, moment, basis, w, raw1, sems,
):
    scales = []
    for side in range(2):
        squares = sums[side]
        for k in range(2 + side, 32, 2):
            squares = squares + sums[k]
        scales.append(lax.rsqrt(squares / COLS + 1e-06))
    first = place[2] == 0
    scale = [jnp.where(first, *scales), jnp.where(first, *scales[::-1])]
    basis[...] = right[...] * scale[0]
    copies = [pltpu.make_async_copy(basis, out_basis, sems.at[0])]
    copies[-1].start()
    blend = momentum[...] + gradient[...].astype(F)
    moment[...] = blend - 0.05 * dot(ortho[...], right[...].astype(B), NT)
    copies.append(pltpu.make_async_copy(moment, out_moment, sems.at[1]))
    copies[-1].start()
    for y in range(4):
        for c, part in ((place[1], half1), (1 - place[1], half2)):
            raw1[pl.ds(pl.multiple_of((2 * y + c) * RR, 16), RR), :] = part[y * RR : (y + 1) * RR, :]
    for half, refs in enumerate(((left0, w0, raw0, weight0), (left1, w1, raw1, weight1))):
        left, packed_w, raw, old = refs
        w[256:, :] = packed_w[:256, :]
        w[:128, :256] = packed_w[256:, :256]
        w[128:256, :256] = packed_w[256:, 256:]
        w[:256, 256:] = jnp.zeros((256, 256), B)
        o = (dot(left[...], w[...], NT) * scale[half]).astype(B)
        r = dot(raw[...], w[...], NT).astype(B)
        update = 0.3 * dot(o, r, NT)
        if half == 0:
            weight[half] = (old[...].astype(F) - update).astype(B)
        else:
            late, wide = update.shape[0] - EARLY, update.shape[1] - N
            weight[half, :EARLY] = (old[...].astype(F) - update[:EARLY]).astype(B)
            low, high = half1[4 * RR : 4 * RR + late, :], half1[4 * RR + late :, :wide]
            weight[half, EARLY:, :N] = (low.astype(F) - update[EARLY:, :N]).astype(B)
            weight[half, EARLY:, N:] = (high.astype(F) - update[EARLY:, N:]).astype(B)
        side = place[2] if half == 0 else 1 - place[2]
        copies.append(pltpu.make_async_copy(weight.at[half], out_rollout.at[side], sems.at[2 + half]))
        copies[-1].start()
        if half == 0:
            copies.append(pltpu.make_async_copy(weight.at[0], out_weight, sems.at[4]))
            copies[-1].start()
    for copy in copies:
        copy.wait()


def exchange(x, axis):
    return lax.all_to_all(x, axis, 0, 0, tiled=True)


def swap(x, axis, bit=1):
    return lax.ppermute(x, axis, [(i, i ^ bit) for i in range(lax.axis_size(axis))])


def body(weights, gradient, momentum, basis):
    place = jnp.stack([lax.axis_index(axis) for axis in ("y", "c", "r")]).astype(jnp.int32)
    place, basis = lax.optimization_barrier((place, basis))
    momentum, gradient = momentum[0], gradient[0]
    part, blend16 = front(momentum, gradient, basis[0])
    part = part.reshape(16, -1, N)
    (copies,) = call(spread_kernel, [(part.shape, B)], name="spread")(exchange(part, TP))
    left = exchange(copies, TP).reshape(-1, N)

    keep_g, keep_r, send = call(
        pieces_kernel,
        [((4, GR, 256), F), ((4, RR, N), F), ((4, RR + GR, N), B)],
        [pltpu.VMEM((8 * RR, N), F), pltpu.VMEM((384, 256), F)],
        smem=1,
        name="pieces",
    )(place, left, blend16)
    got = swap(send, "c")
    left_o = swap(left, "r")
    weight, _ = lax.optimization_barrier((weights[0, :EARLY], left))
    weight_o = swap(weight, "r")
    own_g, own_r, *outs = call(
        join_kernel,
        [((GR, 256), F), ((RR, N), F)] + [((RR + GR, N), B)] * 3,
        smem=1,
        name="join",
    )(place, keep_g, keep_r, got)
    arrived = [swap(x, "y", k + 1) for k, x in enumerate(outs)]
    (piece,) = call(sum_kernel, [((RR + GR, N), B)], name="sum")(own_g, own_r, *arrived)
    late = 2 * (weights.shape[1] - EARLY)
    line, half = call(line_kernel, [((4, RR + GR, N), B), ((4 * RR + late, N), B)], smem=1, name="line")(
        place, piece, *[swap(piece, "y", k) for k in (1, 2, 3)], weights[0]
    )
    line, half, left_o, weight_o = lax.optimization_barrier((line, half, left_o, weight_o))
    other_core = swap(line, "c")
    half_o = swap(half, "r")
    (raw,) = call(rows_kernel, [((8 * RR, N), B)], smem=1, name="rows")(place, line, other_core)

    w16, ortho, right, squares = call(
        solve_kernel,
        [((384, N), B), ((N, N), B), ((8 * RR, N), F), ((1, N), F)],
        [pltpu.VMEM((N, N), F), pltpu.VMEM((N, N), F)],
        smem=1,
        name="solve",
    )(place, line, other_core, left, raw)
    w16, half_o = lax.optimization_barrier((w16, half_o))
    w16_o = swap(w16, "r")
    half_oc = swap(half_o, "c")
    sums = exchange(jnp.broadcast_to(squares[None], (32, 1, N)), ("x", "z", "r"))
    wide, tall = momentum.shape, right.shape
    weight_new, moment_new, basis_new, rollout = call(
        last_kernel,
        [(wide, B), (wide, F), (tall, F), ((2, *wide), B)],
        [pltpu.VMEM((2, *wide), B), pltpu.VMEM(wide, F), pltpu.VMEM(tall, F), pltpu.VMEM((N, N), B)]
        + [pltpu.VMEM((8 * RR, N), B), pltpu.SemaphoreType.DMA((5,))],
        smem=1,
        name="last",
        mib=24,
        out_spec=pl.BlockSpec(memory_space=pl.ANY),
    )(
        place, sums, momentum, gradient, ortho, right, left, w16, raw, weights[0], left_o, w16_o, half_o, half_oc, weight_o
    )
    return weight_new[None], moment_new[None], basis_new[None], rollout


def solution(mesh):
    finer = Mesh(mesh.devices.reshape(4, 2, 2, 8, 2), ("y", "c", "x", "z", "r"))
    split_specs = P("r", FSDP, TP)
    basis_spec = P("r", TP, None)
    return jax.shard_map(
        body,
        mesh=finer,
        in_specs=(split_specs, split_specs, split_specs, basis_spec),
        out_specs=(split_specs, split_specs, basis_spec, P(None, FSDP, TP)),
        check_vma=False,
    )
```

```python
import jax
import jax.numpy as jnp
from jax import lax
from jax.experimental import pallas as pl
from jax.experimental.pallas import tpu as pltpu
from jax.sharding import Mesh
from jax.sharding import PartitionSpec as P

COLS = 14336
TP = ("x", "z")
FSDP = ("y", "c")
F = jnp.float32
B = jnp.bfloat16
N = 512
NB = 128
GRP = 8
GR = 80
RR = 112
EARLY = 384
VMEM = pl.BlockSpec(memory_space=pltpu.VMEM)
SMEM = pl.BlockSpec(memory_space=pltpu.SMEM)


def call(kernel, outs, scratch=(), smem=0, name=None, mib=12, out_spec=VMEM):
    def run(*args):
        return pl.pallas_call(
            kernel,
            out_shape=[jax.ShapeDtypeStruct(s, d) for s, d in outs],
            in_specs=[SMEM] * smem + [VMEM] * (len(args) - smem),
            out_specs=[out_spec] * len(outs),
            scratch_shapes=list(scratch),
            compiler_params=pltpu.CompilerParams(vmem_limit_bytes=mib * 2**20),
            name=name,
        )(*args)

    return run


def dot(p, q, over):
    return lax.dot_general(p, q, (over, ((), ())), preferred_element_type=F)


NN, NT, TN = ((1,), (0,)), ((1,), (1,)), ((0,), (0,))


def halves(x):
    hi = x.astype(B)
    return hi, (x - hi.astype(F)).astype(B)


def dot3(a, b, over):
    ah, al = halves(a)
    bh, bl = halves(b)
    return dot(ah, bh, over) + (dot(ah, bl, over) + dot(al, bh, over))


def total(v):
    while len(v) > 1:
        v = [v[i] + v[i + 1] if i + 1 < len(v) else v[i] for i in range(0, len(v), 2)]
    return v[0]


def factor(rows):
    n, w, b = len(rows), rows[0].shape[1], GRP
    sub = lax.broadcasted_iota(jnp.int32, (8, w), 0)
    lane = lax.broadcasted_iota(jnp.int32, (8, w), 1)
    full = lambda v: jnp.broadcast_to(v, (8, w))
    for p in range(n):
        j = 8 * p
        cols = [full(rows[p][:, j + m : j + m + 1]) for m in range(b)]
        d = [[full(cols[m][i : i + 1, :]) for m in range(i + 1)] for i in range(b)]
        group = (lane >= j) & (lane < j + b)
        own = jnp.where(group, jnp.where(lane == sub + j, 1.0, 0.0), rows[p])
        row = [full(own[m : m + 1, :]) for m in range(b)]
        v = [[None] * b for _ in range(b)]
        low = [[None] * b for _ in range(b)]
        for i in range(b):
            rt = lax.rsqrt(d[i][i])
            for m in range(i + 1, b):
                low[m][i] = d[m][i] * rt
            for m in range(i + 1, b):
                for t in range(i + 1, m + 1):
                    d[m][t] = d[m][t] - low[m][i] * low[t][i]
            v[i][i] = rt
            for t in range(i):
                v[i][t] = -(rt * total([low[i][k] * v[k][t] for k in range(t, i)]))
        r = [total([v[i][m] * row[m] for m in range(i + 1)]) for i in range(b)]
        z = [total([v[i][m] * r[i] for i in range(m, b)]) for m in range(b)]
        for q in range(p + 1, min(p + 2, n)):
            c = [full(rows[q][:, j + m : j + m + 1]) for m in range(b)]
            rows[q] = jnp.where(group, 0.0, rows[q]) - total([c[m] * z[m] for m in range(b)])
        if p + 2 < n:
            far = jnp.concatenate(rows[p + 2 :], axis=0)
            terms = z[0]
            for m in range(1, b):
                terms = jnp.where(sub == m, z[m], terms)
            update = dot3(jnp.where(group[:1], far, 0.0), jnp.concatenate([terms] * (w // 8), axis=0), NN)
            far = jnp.where(group[:1], 0.0, far) - update
            for q in range(p + 2, n):
                rows[q] = far[8 * (q - p - 2) : 8 * (q - p - 1), :]
        y = r[0]
        for i in range(1, b):
            y = jnp.where(sub == i, r[i], y)
        rows[p] = jnp.where(lane < j + b, y, 0.0)
    return rows


def inverse_factor(a_ref, w_ref):
    for lo in range(0, N, NB):
        hi = lo + NB
        rows = [a_ref[lo + 8 * p : lo + 8 * p + 8, lo:hi] for p in range(NB // 8)]
        wkk = jnp.concatenate(factor(rows), axis=0)
        w_ref[lo:hi, lo:hi] = wkk
        if hi < N:
            w_ref[lo:hi, hi:] = jnp.zeros((NB, N - hi), F)
        if lo > 0:
            w_ref[lo:hi, :lo] = dot3(wkk, w_ref[lo:hi, :lo], NN)
        if hi < N:
            r = dot3(wkk, a_ref[lo:hi, hi:], NN)
            for s in range(hi, N, NB):
                a_ref[s : s + NB, s:] = a_ref[s : s + NB, s:] - dot3(r[:, s - hi : s - hi + NB], r[:, s - hi :], TN)
            upd = dot3(r, w_ref[lo:hi, :hi], TN)
            if lo > 0:
                w_ref[hi:, :lo] = w_ref[hi:, :lo] - upd[:, :lo]
            w_ref[hi:, lo:hi] = -upd[:, lo:]


def front_kernel(momentum, gradient, basis, part, blend, m_ref, g_ref, b_ref, sems):
    steps = 4
    step = m_ref.shape[0] // steps
    copies = [pltpu.make_async_copy(basis, b_ref, sems.at[2 * steps])]
    for k in range(steps):
        rows = pl.ds(k * step, step)
        copies.append(pltpu.make_async_copy(momentum.at[rows], m_ref.at[rows], sems.at[2 * k]))
        copies.append(pltpu.make_async_copy(gradient.at[rows], g_ref.at[rows], sems.at[2 * k + 1]))
    for copy in copies:
        copy.start()
    copies[0].wait()
    basis16 = b_ref[...].astype(B)
    for k in range(steps):
        copies[2 * k + 1].wait()
        copies[2 * k + 2].wait()
        rows = pl.ds(k * step, step)
        x = (m_ref[rows] + g_ref[rows].astype(F)).astype(B)
        blend[rows] = x
        part[rows] = dot(x, basis16, NN).astype(B)


def front(momentum, gradient, basis):
    rows, cols = momentum.shape
    return pl.pallas_call(
        front_kernel,
        out_shape=[jax.ShapeDtypeStruct((rows, N), B), jax.ShapeDtypeStruct((rows, cols), B)],
        in_specs=[pl.BlockSpec(memory_space=pltpu.HBM)] * 3,
        out_specs=[VMEM] * 2,
        scratch_shapes=[
            pltpu.VMEM((rows, cols), F),
            pltpu.VMEM((rows, cols), B),
            pltpu.VMEM((cols, N), F),
            pltpu.SemaphoreType.DMA((9,)),
        ],
        compiler_params=pltpu.CompilerParams(vmem_limit_bytes=60 * 2**20),
        name="front",
    )(momentum, gradient, basis)


def spread_kernel(pieces, out):
    share = pieces[0].astype(F)
    for k in range(1, pieces.shape[0]):
        share = share + pieces[k].astype(F)
    share = share.astype(B)
    for k in range(out.shape[0]):
        out[k] = share


def pieces_kernel(place, left_ref, blend_ref, keep_g, keep_r, send, right_scr, part):
    right_scr[...] = dot(blend_ref[...], left_ref[...], TN)
    for mine in (True, False):
        c = place[1] if mine else 1 - place[1]
        wide = left_ref[:, pl.ds(pl.multiple_of(c * 256, 256), 256)]
        narrow = left_ref[:, pl.ds(pl.multiple_of(c * 128, 128), 128)]
        part[:128, :] = dot(wide[:, :128], wide, TN)
        corner = dot(wide[:, 128:], wide[:, 128:], TN)
        part[128:192, :128] = corner[:64, :]
        part[128:192, 128:] = corner[64:, :]
        part[192:, :] = dot(narrow, left_ref[:, 256:], TN)
        for y in range(4):
            g = part[y * GR : (y + 1) * GR, :]
            r = right_scr[pl.ds(pl.multiple_of((2 * y + c) * RR, 16), RR), :]
            if mine:
                keep_g[y] = g
                keep_r[y] = r
            else:
                packed(send.at[y], g, r)


def packed(out, g, r):
    gh, gl = halves(g)
    out[:RR, :] = r.astype(B)
    out[RR:, :256] = gh
    out[RR:, 256:] = gl


def gram_of(ref):
    return ref[RR:, :256].astype(F) + ref[RR:, 256:].astype(F)


def join_kernel(place, keep_g, keep_r, got, own_g, own_r, one, two, three):
    for k, out in enumerate((None, one, two, three)):
        y = place[0] ^ k
        r = keep_r[y] + got[y, :RR, :].astype(F)
        g = keep_g[y] + gram_of(got.at[y])
        if out is None:
            own_g[...] = g
            own_r[...] = r
        else:
            packed(out, g, r)


def sum_kernel(own_g, own_r, one, two, three, out):
    g, r = own_g[...], own_r[...]
    for got in (one, two, three):
        r = r + got[:RR, :].astype(F)
        g = g + gram_of(got)
    packed(out, g, r)


def line_kernel(place, own, one, two, three, weight, out, half):
    late, wide = weight.shape[0] - EARLY, weight.shape[1] - N
    for k, got in enumerate((own, one, two, three)):
        y = place[0] ^ k
        out[y] = got[...]
        half[pl.ds(pl.multiple_of(y * RR, 16), RR), :] = got[:RR, :]
    half[4 * RR : 4 * RR + late, :] = weight[EARLY:, :N]
    half[4 * RR + late :, :wide] = weight[EARLY:, N:]
    half[4 * RR + late :, wide:] = jnp.zeros((late, N - wide), B)


def rows_kernel(place, own, got, right):
    for y in range(4):
        for c, part in ((place[1], own), (1 - place[1], got)):
            right[pl.ds(pl.multiple_of((2 * y + c) * RR, 16), RR), :] = part[y, :RR, :]


def solve_kernel(place, own, got, left, right_in, w16, ortho, right, squares, a, w):
    for c, part in ((place[1], own), (1 - place[1], got)):
        at = lambda first, count: pl.ds(pl.multiple_of(first, 16), count)
        square = pl.ds(pl.multiple_of(c * 256, 256), 256)
        corner = pl.ds(pl.multiple_of(c * 256 + 128, 128), 128)
        g = [gram_of(part.at[y]) for y in range(4)]
        a[at(c * 256, 80), square] = g[0]
        a[at(c * 256 + 80, 48), square] = g[1][:48, :]
        for first, rows in ((128, g[1][48:, :]), (160, g[2][:32, :])):
            a[at(c * 256 + first, 32), corner] = rows[:, :128]
            a[at(c * 256 + first + 64, 32), corner] = rows[:, 128:]
        a[at(c * 128, 48), 256:] = g[2][32:, :]
        a[at(c * 128 + 48, 80), 256:] = g[3]
    inverse_factor(a, w)
    wh, wl = halves(w[...])
    w16[:256, :] = wh[256:, :]
    w16[256:, :256] = wh[:128, :256]
    w16[256:, 256:] = wh[128:256, :256]
    ortho[...] = (dot(left[...], wh, NT) + dot(left[...], wl, NT)).astype(B)
    r = dot(right_in[...], wh, NT) + dot(right_in[...], wl, NT)
    right[...] = r
    squares[...] = jnp.sum(r * r, axis=0, keepdims=True)


def last_kernel(
    place, sums, momentum, gradient, ortho, right, left0, w0, raw0, weight0, left1, w1, half1, half2, weight1,
    out_weight, out_moment, out_basis, out_rollout, weight, moment, basis, w, raw1, sems,
):
    scales = []
    for side in range(2):
        squares = sums[side]
        for k in range(2 + side, 32, 2):
            squares = squares + sums[k]
        scales.append(lax.rsqrt(squares / COLS + 1e-06))
    first = place[2] == 0
    scale = [jnp.where(first, *scales), jnp.where(first, *scales[::-1])]
    basis[...] = right[...] * scale[0]
    copies = [pltpu.make_async_copy(basis, out_basis, sems.at[0])]
    copies[-1].start()
    blend = momentum[...] + gradient[...].astype(F)
    moment[...] = blend - 0.05 * dot(ortho[...], right[...].astype(B), NT)
    copies.append(pltpu.make_async_copy(moment, out_moment, sems.at[1]))
    copies[-1].start()
    for y in range(4):
        for c, part in ((place[1], half1), (1 - place[1], half2)):
            raw1[pl.ds(pl.multiple_of((2 * y + c) * RR, 16), RR), :] = part[y * RR : (y + 1) * RR, :]
    for half, refs in enumerate(((left0, w0, raw0, weight0), (left1, w1, raw1, weight1))):
        left, packed_w, raw, old = refs
        w[256:, :] = packed_w[:256, :]
        w[:128, :256] = packed_w[256:, :256]
        w[128:256, :256] = packed_w[256:, 256:]
        w[:256, 256:] = jnp.zeros((256, 256), B)
        o = (dot(left[...], w[...], NT) * scale[half]).astype(B)
        r = dot(raw[...], w[...], NT).astype(B)
        update = 0.3 * dot(o, r, NT)
        if half == 0:
            weight[half] = (old[...].astype(F) - update).astype(B)
        else:
            late, wide = update.shape[0] - EARLY, update.shape[1] - N
            weight[half, :EARLY] = (old[...].astype(F) - update[:EARLY]).astype(B)
            low, high = half1[4 * RR : 4 * RR + late, :], half1[4 * RR + late :, :wide]
            weight[half, EARLY:, :N] = (low.astype(F) - update[EARLY:, :N]).astype(B)
            weight[half, EARLY:, N:] = (high.astype(F) - update[EARLY:, N:]).astype(B)
        side = place[2] if half == 0 else 1 - place[2]
        copies.append(pltpu.make_async_copy(weight.at[half], out_rollout.at[side], sems.at[2 + half]))
        copies[-1].start()
        if half == 0:
            copies.append(pltpu.make_async_copy(weight.at[0], out_weight, sems.at[4]))
            copies[-1].start()
    for copy in copies:
        copy.wait()


def exchange(x, axis):
    return lax.all_to_all(x, axis, 0, 0, tiled=True)


def swap(x, axis, bit=1):
    return lax.ppermute(x, axis, [(i, i ^ bit) for i in range(lax.axis_size(axis))])


def body(weights, gradient, momentum, basis):
    place = jnp.stack([lax.axis_index(axis) for axis in ("y", "c", "r")]).astype(jnp.int32)
    place, basis = lax.optimization_barrier((place, basis))
    momentum, gradient = momentum[0], gradient[0]
    part, blend16 = front(momentum, gradient, basis[0])
    part = part.reshape(16, -1, N)
    (copies,) = call(spread_kernel, [(part.shape, B)], name="spread")(exchange(part, TP))
    left = exchange(copies, TP).reshape(-1, N)

    keep_g, keep_r, send = call(
        pieces_kernel,
        [((4, GR, 256), F), ((4, RR, N), F), ((4, RR + GR, N), B)],
        [pltpu.VMEM((8 * RR, N), F), pltpu.VMEM((4 * GR, 256), F)],
        smem=1,
        name="pieces",
    )(place, left, blend16)
    got = swap(send, "c")
    left_o = swap(left, "r")
    weight, _ = lax.optimization_barrier((weights[0, :EARLY], left))
    weight_o = swap(weight, "r")
    own_g, own_r, *outs = call(
        join_kernel,
        [((GR, 256), F), ((RR, N), F)] + [((RR + GR, N), B)] * 3,
        smem=1,
        name="join",
    )(place, keep_g, keep_r, got)
    arrived = [swap(x, "y", k + 1) for k, x in enumerate(outs)]
    (piece,) = call(sum_kernel, [((RR + GR, N), B)], name="sum")(own_g, own_r, *arrived)
    late = 2 * (weights.shape[1] - EARLY)
    line, half = call(line_kernel, [((4, RR + GR, N), B), ((4 * RR + late, N), B)], smem=1, name="line")(
        place, piece, *[swap(piece, "y", k) for k in (1, 2, 3)], weights[0]
    )
    line, half, left_o, weight_o = lax.optimization_barrier((line, half, left_o, weight_o))
    other_core = swap(line, "c")
    half_o = swap(half, "r")
    (raw,) = call(rows_kernel, [((8 * RR, N), B)], smem=1, name="rows")(place, line, other_core)

    w16, ortho, right, squares = call(
        solve_kernel,
        [((384, N), B), ((N, N), B), ((8 * RR, N), F), ((1, N), F)],
        [pltpu.VMEM((N, N), F), pltpu.VMEM((N, N), F)],
        smem=1,
        name="solve",
    )(place, line, other_core, left, raw)
    w16, half_o = lax.optimization_barrier((w16, half_o))
    w16_o = swap(w16, "r")
    half_oc = swap(half_o, "c")
    sums = exchange(jnp.broadcast_to(squares[None], (32, 1, N)), ("x", "z", "r"))
    wide, tall = momentum.shape, right.shape
    weight_new, moment_new, basis_new, rollout = call(
        last_kernel,
        [(wide, B), (wide, F), (tall, F), ((2, *wide), B)],
        [pltpu.VMEM((2, *wide), B), pltpu.VMEM(wide, F), pltpu.VMEM(tall, F), pltpu.VMEM((N, N), B)]
        + [pltpu.VMEM((8 * RR, N), B), pltpu.SemaphoreType.DMA((5,))],
        smem=1,
        name="last",
        mib=24,
        out_spec=pl.BlockSpec(memory_space=pl.ANY),
    )(
        place, sums, momentum, gradient, ortho, right, left, w16, raw, weights[0], left_o, w16_o, half_o, half_oc, weight_o
    )
    return weight_new[None], moment_new[None], basis_new[None], rollout


def solution(mesh):
    finer = Mesh(mesh.devices.reshape(4, 2, 2, 8, 2), ("y", "c", "x", "z", "r"))
    split_specs = P("r", FSDP, TP)
    basis_spec = P("r", TP, None)
    return jax.shard_map(
        body,
        mesh=finer,
        in_specs=(split_specs, split_specs, split_specs, basis_spec),
        out_specs=(split_specs, split_specs, basis_spec, P(None, FSDP, TP)),
        check_vma=False,
    )
```

```python
import jax
import jax.numpy as jnp
from jax import lax
from jax.experimental import pallas as pl
from jax.experimental.pallas import tpu as pltpu
from jax.sharding import Mesh
from jax.sharding import PartitionSpec as P

COLS = 14336
TP = ("x", "z")
FSDP = ("y", "c")
F = jnp.float32
B = jnp.bfloat16
N = 512
NB = 128
GRP = 8
GR = 80
RR = 112
EARLY = 320
VMEM = pl.BlockSpec(memory_space=pltpu.VMEM)
SMEM = pl.BlockSpec(memory_space=pltpu.SMEM)


def call(kernel, outs, scratch=(), smem=0, name=None, mib=12, out_spec=VMEM):
    def run(*args):
        return pl.pallas_call(
            kernel,
            out_shape=[jax.ShapeDtypeStruct(s, d) for s, d in outs],
            in_specs=[SMEM] * smem + [VMEM] * (len(args) - smem),
            out_specs=[out_spec] * len(outs),
            scratch_shapes=list(scratch),
            compiler_params=pltpu.CompilerParams(vmem_limit_bytes=mib * 2**20),
            name=name,
        )(*args)

    return run


def dot(p, q, over):
    return lax.dot_general(p, q, (over, ((), ())), preferred_element_type=F)


NN, NT, TN = ((1,), (0,)), ((1,), (1,)), ((0,), (0,))


def halves(x):
    hi = x.astype(B)
    return hi, (x - hi.astype(F)).astype(B)


def dot3(a, b, over):
    ah, al = halves(a)
    bh, bl = halves(b)
    return dot(ah, bh, over) + (dot(ah, bl, over) + dot(al, bh, over))


def total(v):
    while len(v) > 1:
        v = [v[i] + v[i + 1] if i + 1 < len(v) else v[i] for i in range(0, len(v), 2)]
    return v[0]


def factor(rows):
    n, w, b = len(rows), rows[0].shape[1], GRP
    sub = lax.broadcasted_iota(jnp.int32, (8, w), 0)
    lane = lax.broadcasted_iota(jnp.int32, (8, w), 1)
    full = lambda v: jnp.broadcast_to(v, (8, w))
    for p in range(n):
        j = 8 * p
        cols = [full(rows[p][:, j + m : j + m + 1]) for m in range(b)]
        d = [[full(cols[m][i : i + 1, :]) for m in range(i + 1)] for i in range(b)]
        group = (lane >= j) & (lane < j + b)
        own = jnp.where(group, jnp.where(lane == sub + j, 1.0, 0.0), rows[p])
        row = [full(own[m : m + 1, :]) for m in range(b)]
        v = [[None] * b for _ in range(b)]
        low = [[None] * b for _ in range(b)]
        for i in range(b):
            rt = lax.rsqrt(d[i][i])
            for m in range(i + 1, b):
                low[m][i] = d[m][i] * rt
            for m in range(i + 1, b):
                for t in range(i + 1, m + 1):
                    d[m][t] = d[m][t] - low[m][i] * low[t][i]
            v[i][i] = rt
            for t in range(i):
                v[i][t] = -(rt * total([low[i][k] * v[k][t] for k in range(t, i)]))
        r = [total([v[i][m] * row[m] for m in range(i + 1)]) for i in range(b)]
        z = [total([v[i][m] * r[i] for i in range(m, b)]) for m in range(b)]
        for q in range(p + 1, min(p + 2, n)):
            c = [full(rows[q][:, j + m : j + m + 1]) for m in range(b)]
            rows[q] = jnp.where(group, 0.0, rows[q]) - total([c[m] * z[m] for m in range(b)])
        if p + 2 < n:
            far = jnp.concatenate(rows[p + 2 :], axis=0)
            terms = z[0]
            for m in range(1, b):
                terms = jnp.where(sub == m, z[m], terms)
            update = dot3(jnp.where(group[:1], far, 0.0), jnp.concatenate([terms] * (w // 8), axis=0), NN)
            far = jnp.where(group[:1], 0.0, far) - update
            for q in range(p + 2, n):
                rows[q] = far[8 * (q - p - 2) : 8 * (q - p - 1), :]
        y = r[0]
        for i in range(1, b):
            y = jnp.where(sub == i, r[i], y)
        rows[p] = jnp.where(lane < j + b, y, 0.0)
    return rows


def inverse_factor(a_ref, w_ref):
    for lo in range(0, N, NB):
        hi = lo + NB
        rows = [a_ref[lo + 8 * p : lo + 8 * p + 8, lo:hi] for p in range(NB // 8)]
        wkk = jnp.concatenate(factor(rows), axis=0)
        w_ref[lo:hi, lo:hi] = wkk
        if hi < N:
            w_ref[lo:hi, hi:] = jnp.zeros((NB, N - hi), F)
        if lo > 0:
            w_ref[lo:hi, :lo] = dot3(wkk, w_ref[lo:hi, :lo], NN)
        if hi < N:
            r = dot3(wkk, a_ref[lo:hi, hi:], NN)
            for s in range(hi, N, NB):
                a_ref[s : s + NB, s:] = a_ref[s : s + NB, s:] - dot3(r[:, s - hi : s - hi + NB], r[:, s - hi :], TN)
            upd = dot3(r, w_ref[lo:hi, :hi], TN)
            if lo > 0:
                w_ref[hi:, :lo] = w_ref[hi:, :lo] - upd[:, :lo]
            w_ref[hi:, lo:hi] = -upd[:, lo:]


def front_kernel(momentum, gradient, basis, part, blend, m_ref, g_ref, b_ref, sems):
    steps = 4
    step = m_ref.shape[0] // steps
    copies = [pltpu.make_async_copy(basis, b_ref, sems.at[2 * steps])]
    for k in range(steps):
        rows = pl.ds(k * step, step)
        copies.append(pltpu.make_async_copy(momentum.at[rows], m_ref.at[rows], sems.at[2 * k]))
        copies.append(pltpu.make_async_copy(gradient.at[rows], g_ref.at[rows], sems.at[2 * k + 1]))
    for copy in copies:
        copy.start()
    copies[0].wait()
    basis16 = b_ref[...].astype(B)
    for k in range(steps):
        copies[2 * k + 1].wait()
        copies[2 * k + 2].wait()
        rows = pl.ds(k * step, step)
        x = (m_ref[rows] + g_ref[rows].astype(F)).astype(B)
        blend[rows] = x
        part[rows] = dot(x, basis16, NN).astype(B)


def front(momentum, gradient, basis):
    rows, cols = momentum.shape
    return pl.pallas_call(
        front_kernel,
        out_shape=[jax.ShapeDtypeStruct((rows, N), B), jax.ShapeDtypeStruct((rows, cols), B)],
        in_specs=[pl.BlockSpec(memory_space=pltpu.HBM)] * 3,
        out_specs=[VMEM] * 2,
        scratch_shapes=[
            pltpu.VMEM((rows, cols), F),
            pltpu.VMEM((rows, cols), B),
            pltpu.VMEM((cols, N), F),
            pltpu.SemaphoreType.DMA((9,)),
        ],
        compiler_params=pltpu.CompilerParams(vmem_limit_bytes=60 * 2**20),
        name="front",
    )(momentum, gradient, basis)


def spread_kernel(pieces, out):
    share = pieces[0].astype(F)
    for k in range(1, pieces.shape[0]):
        share = share + pieces[k].astype(F)
    share = share.astype(B)
    for k in range(out.shape[0]):
        out[k] = share


def pieces_kernel(place, left_ref, blend_ref, keep_g, keep_r, send, right_scr, part):
    right_scr[...] = dot(blend_ref[...], left_ref[...], TN)
    for mine in (True, False):
        c = place[1] if mine else 1 - place[1]
        wide = left_ref[:, pl.ds(pl.multiple_of(c * 256, 256), 256)]
        narrow = left_ref[:, pl.ds(pl.multiple_of(c * 128, 128), 128)]
        part[:128, :] = dot(wide[:, :128], wide, TN)
        corner = dot(wide[:, 128:], wide[:, 128:], TN)
        part[128:192, :128] = corner[:64, :]
        part[128:192, 128:] = corner[64:, :]
        part[192:, :] = dot(narrow, left_ref[:, 256:], TN)
        for y in range(4):
            g = part[y * GR : (y + 1) * GR, :]
            r = right_scr[pl.ds(pl.multiple_of((2 * y + c) * RR, 16), RR), :]
            if mine:
                keep_g[y] = g
                keep_r[y] = r
            else:
                packed(send.at[y], g, r)


def packed(out, g, r):
    gh, gl = halves(g)
    out[:RR, :] = r.astype(B)
    out[RR:, :256] = gh
    out[RR:, 256:] = gl


def gram_of(ref):
    return ref[RR:, :256].astype(F) + ref[RR:, 256:].astype(F)


def join_kernel(place, keep_g, keep_r, got, own_g, own_r, one, two, three):
    for k, out in enumerate((None, one, two, three)):
        y = place[0] ^ k
        r = keep_r[y] + got[y, :RR, :].astype(F)
        g = keep_g[y] + gram_of(got.at[y])
        if out is None:
            own_g[...] = g
            own_r[...] = r
        else:
            packed(out, g, r)


def sum_kernel(own_g, own_r, one, two, three, out):
    g, r = own_g[...], own_r[...]
    for got in (one, two, three):
        r = r + got[:RR, :].astype(F)
        g = g + gram_of(got)
    packed(out, g, r)


def line_kernel(place, own, one, two, three, weight, out, half):
    late, wide = weight.shape[0] - EARLY, weight.shape[1] - N
    for k, got in enumerate((own, one, two, three)):
        y = place[0] ^ k
        out[y] = got[...]
        half[pl.ds(pl.multiple_of(y * RR, 16), RR), :] = got[:RR, :]
    half[4 * RR : 4 * RR + late, :] = weight[EARLY:, :N]
    half[4 * RR + late :, :wide] = weight[EARLY:, N:]
    half[4 * RR + late :, wide:] = jnp.zeros((late, N - wide), B)


def rows_kernel(place, own, got, right):
    for y in range(4):
        for c, part in ((place[1], own), (1 - place[1], got)):
            right[pl.ds(pl.multiple_of((2 * y + c) * RR, 16), RR), :] = part[y, :RR, :]


def solve_kernel(place, own, got, left, right_in, w16, ortho, right, squares, a, w):
    for c, part in ((place[1], own), (1 - place[1], got)):
        at = lambda first, count: pl.ds(pl.multiple_of(first, 16), count)
        square = pl.ds(pl.multiple_of(c * 256, 256), 256)
        corner = pl.ds(pl.multiple_of(c * 256 + 128, 128), 128)
        g = [gram_of(part.at[y]) for y in range(4)]
        a[at(c * 256, 80), square] = g[0]
        a[at(c * 256 + 80, 48), square] = g[1][:48, :]
        for first, rows in ((128, g[1][48:, :]), (160, g[2][:32, :])):
            a[at(c * 256 + first, 32), corner] = rows[:, :128]
            a[at(c * 256 + first + 64, 32), corner] = rows[:, 128:]
        a[at(c * 128, 48), 256:] = g[2][32:, :]
        a[at(c * 128 + 48, 80), 256:] = g[3]
    inverse_factor(a, w)
    wh, wl = halves(w[...])
    w16[:256, :] = wh[256:, :]
    w16[256:, :256] = wh[:128, :256]
    w16[256:, 256:] = wh[128:256, :256]
    ortho[...] = (dot(left[...], wh, NT) + dot(left[...], wl, NT)).astype(B)
    r = dot(right_in[...], wh, NT) + dot(right_in[...], wl, NT)
    right[...] = r
    squares[...] = jnp.sum(r * r, axis=0, keepdims=True)


def last_kernel(
    place, sums, momentum, gradient, ortho, right, left0, w0, raw0, weight0, left1, w1, half1, half2, weight1,
    out_weight, out_moment, out_basis, out_rollout, weight, moment, basis, w, raw1, sems,
):
    scales = []
    for side in range(2):
        squares = sums[side]
        for k in range(2 + side, 32, 2):
            squares = squares + sums[k]
        scales.append(lax.rsqrt(squares / COLS + 1e-06))
    first = place[2] == 0
    scale = [jnp.where(first, *scales), jnp.where(first, *scales[::-1])]
    basis[...] = right[...] * scale[0]
    copies = [pltpu.make_async_copy(basis, out_basis, sems.at[0])]
    copies[-1].start()
    blend = momentum[...] + gradient[...].astype(F)
    moment[...] = blend - 0.05 * dot(ortho[...], right[...].astype(B), NT)
    copies.append(pltpu.make_async_copy(moment, out_moment, sems.at[1]))
    copies[-1].start()
    for y in range(4):
        for c, part in ((place[1], half1), (1 - place[1], half2)):
            raw1[pl.ds(pl.multiple_of((2 * y + c) * RR, 16), RR), :] = part[y * RR : (y + 1) * RR, :]
    for half, refs in enumerate(((left0, w0, raw0, weight0), (left1, w1, raw1, weight1))):
        left, packed_w, raw, old = refs
        w[256:, :] = packed_w[:256, :]
        w[:128, :256] = packed_w[256:, :256]
        w[128:256, :256] = packed_w[256:, 256:]
        w[:256, 256:] = jnp.zeros((256, 256), B)
        o = (dot(left[...], w[...], NT) * scale[half]).astype(B)
        r = dot(raw[...], w[...], NT).astype(B)
        update = 0.3 * dot(o, r, NT)
        if half == 0:
            weight[half] = (old[...].astype(F) - update).astype(B)
        else:
            late, wide = update.shape[0] - EARLY, update.shape[1] - N
            weight[half, :EARLY] = (old[...].astype(F) - update[:EARLY]).astype(B)
            low, high = half1[4 * RR : 4 * RR + late, :], half1[4 * RR + late :, :wide]
            weight[half, EARLY:, :N] = (low.astype(F) - update[EARLY:, :N]).astype(B)
            weight[half, EARLY:, N:] = (high.astype(F) - update[EARLY:, N:]).astype(B)
        side = place[2] if half == 0 else 1 - place[2]
        copies.append(pltpu.make_async_copy(weight.at[half], out_rollout.at[side], sems.at[2 + half]))
        copies[-1].start()
        if half == 0:
            copies.append(pltpu.make_async_copy(weight.at[0], out_weight, sems.at[4]))
            copies[-1].start()
    for copy in copies:
        copy.wait()


def exchange(x, axis):
    return lax.all_to_all(x, axis, 0, 0, tiled=True)


def swap(x, axis, bit=1):
    return lax.ppermute(x, axis, [(i, i ^ bit) for i in range(lax.axis_size(axis))])


def body(weights, gradient, momentum, basis):
    place = jnp.stack([lax.axis_index(axis) for axis in ("y", "c", "r")]).astype(jnp.int32)
    place, basis = lax.optimization_barrier((place, basis))
    momentum, gradient = momentum[0], gradient[0]
    part, blend16 = front(momentum, gradient, basis[0])
    part = part.reshape(16, -1, N)
    (copies,) = call(spread_kernel, [(part.shape, B)], name="spread")(exchange(part, TP))
    left = exchange(copies, TP).reshape(-1, N)

    keep_g, keep_r, send = call(
        pieces_kernel,
        [((4, GR, 256), F), ((4, RR, N), F), ((4, RR + GR, N), B)],
        [pltpu.VMEM((8 * RR, N), F), pltpu.VMEM((4 * GR, 256), F)],
        smem=1,
        name="pieces",
    )(place, left, blend16)
    got = swap(send, "c")
    left_o = swap(left, "r")
    weight, _ = lax.optimization_barrier((weights[0, :EARLY], left))
    weight_o = swap(weight, "r")
    own_g, own_r, *outs = call(
        join_kernel,
        [((GR, 256), F), ((RR, N), F)] + [((RR + GR, N), B)] * 3,
        smem=1,
        name="join",
    )(place, keep_g, keep_r, got)
    arrived = [swap(x, "y", k + 1) for k, x in enumerate(outs)]
    (piece,) = call(sum_kernel, [((RR + GR, N), B)], name="sum")(own_g, own_r, *arrived)
    late = 2 * (weights.shape[1] - EARLY)
    line, half = call(line_kernel, [((4, RR + GR, N), B), ((4 * RR + late, N), B)], smem=1, name="line")(
        place, piece, *[swap(piece, "y", k) for k in (1, 2, 3)], weights[0]
    )
    line, half, left_o, weight_o = lax.optimization_barrier((line, half, left_o, weight_o))
    other_core = swap(line, "c")
    half_o = swap(half, "r")
    (raw,) = call(rows_kernel, [((8 * RR, N), B)], smem=1, name="rows")(place, line, other_core)

    w16, ortho, right, squares = call(
        solve_kernel,
        [((384, N), B), ((N, N), B), ((8 * RR, N), F), ((1, N), F)],
        [pltpu.VMEM((N, N), F), pltpu.VMEM((N, N), F)],
        smem=1,
        name="solve",
    )(place, line, other_core, left, raw)
    w16, half_o = lax.optimization_barrier((w16, half_o))
    w16_o = swap(w16, "r")
    half_oc = swap(half_o, "c")
    sums = exchange(jnp.broadcast_to(squares[None], (32, 1, N)), ("x", "z", "r"))
    wide, tall = momentum.shape, right.shape
    weight_new, moment_new, basis_new, rollout = call(
        last_kernel,
        [(wide, B), (wide, F), (tall, F), ((2, *wide), B)],
        [pltpu.VMEM((2, *wide), B), pltpu.VMEM(wide, F), pltpu.VMEM(tall, F), pltpu.VMEM((N, N), B)]
        + [pltpu.VMEM((8 * RR, N), B), pltpu.SemaphoreType.DMA((5,))],
        smem=1,
        name="last",
        mib=24,
        out_spec=pl.BlockSpec(memory_space=pl.ANY),
    )(
        place, sums, momentum, gradient, ortho, right, left, w16, raw, weights[0], left_o, w16_o, half_o, half_oc, weight_o
    )
    return weight_new[None], moment_new[None], basis_new[None], rollout


def solution(mesh):
    finer = Mesh(mesh.devices.reshape(4, 2, 2, 8, 2), ("y", "c", "x", "z", "r"))
    split_specs = P("r", FSDP, TP)
    basis_spec = P("r", TP, None)
    return jax.shard_map(
        body,
        mesh=finer,
        in_specs=(split_specs, split_specs, split_specs, basis_spec),
        out_specs=(split_specs, split_specs, basis_spec, P(None, FSDP, TP)),
        check_vma=False,
    )
```
